32 devices in a mesh: frame: 8 (over y, x, core), row: 4 (over z).
Axes of the slice: x: 2, y: 2, z: 4, core: 2. Of those that a mesh axis runs over, the one named last changes fastest.
Arguments:
- query_tok: bfloat16 [8, 32, 16, 2560], P('frame', 'row'), may hold values from -6 to 6
- key_tok: bfloat16 [8, 32, 16, 2560], P('frame', 'row'), may hold values from -6 to 6
- value_tok: bfloat16 [8, 32, 16, 2560], P('frame', 'row'), may hold values from -6 to 6
- grad_out: bfloat16 [8, 32, 16, 2560], P('frame', 'row'), may hold values from -6 to 6
- head_reach: int32 [20], replicated, may hold values from 0 to 1
- tile_offset: int32 [8, 8], P(None, 'row'), may hold values from -1 to 0
Outputs:
- grad_query: bfloat16 [8, 32, 16, 2560], P('frame', 'row')
- grad_key: bfloat16 [8, 32, 16, 2560], P('frame', 'row')
- grad_value: bfloat16 [8, 32, 16, 2560], P('frame', 'row')
The draws below stay inside these ranges and needn't reach their ends.
All inputs are finite; a program needn't handle non-finite values.
Results may differ from the reference program's by a relative error of at most 0.011.
Values may be sent and summed in bfloat16 or wider, within the bound.
A program may use at most 64 MiB of HBM per device.

```python
import math
import jax
import jax.numpy as jnp
from jax import lax

HEADS = 20
HEAD_DIM = 128
ROWS_DEV = 8
COLS = 16
FRAMES = 8
ROWS = 32


def drawn(key, which):
    shape = (FRAMES, ROWS, COLS, HEADS * HEAD_DIM)
    own_key = jax.random.fold_in(key, 101 + which)
    values = jnp.clip(jax.random.normal(own_key, shape, jnp.float32), -5.0, 5.0)
    return values.astype(jnp.bfloat16)


def draw_query_tok(key, part):
    return drawn(key, 0)


def draw_key_tok(key, part):
    return drawn(key, 1)


def touch_ends(values, key, smallest, top_value):
    dims = values.shape
    place = [jax.random.randint(jax.random.fold_in(key, axis), (), 0, dims[axis]) for axis in range(len(dims))]
    values = values.at[tuple(place)].set(smallest)
    longest = dims.index(max(dims))
    place[longest] = (place[longest] + 1) % dims[longest]
    return values.at[tuple(place)].set(top_value)


def shard_levels(key, dims, shards, smallest, largest):
    level, own = 1.0, jax.random.fold_in(key, 6)
    for dim, blocks in shards:
        heights = jnp.exp(jax.random.uniform(jax.random.fold_in(own, dim), (blocks,), jnp.float32, smallest / len(shards), largest / len(shards)))
        level = level * jnp.repeat(heights, dims[dim] // blocks).reshape([-1 if axis == dim else 1 for axis in range(len(dims))])
    return level


def noise(rng, extent, scale, limit, pieces=(), kind=jnp.bfloat16):
    values = scale * jax.random.normal(rng, extent, jnp.float32)
    if pieces:
        values = values * shard_levels(rng, extent, pieces, -0.22, 0.18)
    return jnp.clip(values, -limit, limit).astype(kind)


def setup_inputs(seed: int = 0) -> dict:
    arg_keys = jax.random.split(jax.random.key(seed), 7)
    return {
        "query_tok": draw_query_tok(jax.random.fold_in(arg_keys[6], 71), 0),
        "key_tok": draw_key_tok(jax.random.fold_in(arg_keys[6], 71), 0),
        "value_tok": noise(arg_keys[2], (FRAMES, ROWS, COLS, HEADS * HEAD_DIM), 1.0, 6.0, ((0, 8), (1, 4))),
        "grad_out": noise(arg_keys[3], (FRAMES, ROWS, COLS, HEADS * HEAD_DIM), 1.0, 6.0, ((0, 8), (1, 4))),
        "head_reach": touch_ends(jax.random.randint(arg_keys[4], (HEADS,), 0, 2), jax.random.fold_in(arg_keys[4], 1), 0, 1).astype(jnp.int32),
        "tile_offset": touch_ends(jax.random.randint(arg_keys[5], (FRAMES, ROWS // 4), -1, 1), jax.random.fold_in(arg_keys[5], 1), -1, 0).astype(jnp.int32),
    }


def build_windows(padded):
    frame_pad = padded.shape[0]
    rows_in = padded.shape[1] - 4
    tiles = rows_in // 4
    width = padded.shape[2]
    trailing = padded.shape[3:]
    upper_part = padded[:, 0:rows_in].reshape((frame_pad, tiles, 4 * width) + trailing)
    lower_part = padded[:, 4:rows_in + 4].reshape((frame_pad, tiles, 4, width) + trailing)[:, :, 0:2]
    lower_part = lower_part.reshape((frame_pad, tiles, 2 * width) + trailing)
    return jnp.concatenate([upper_part, lower_part], axis=2)

def fold_windows(window_grad, width):
    frame_pad, tiles = (window_grad.shape[0], window_grad.shape[1])
    trailing = window_grad.shape[3:]
    rows_in = 4 * tiles
    tail = [(0, 0)] * len(trailing)
    first = window_grad[:, :, 0:4 * width].reshape((frame_pad, rows_in, width) + trailing)
    second = window_grad[:, :, 4 * width:].reshape((frame_pad, tiles, 2, width) + trailing)
    second = jnp.pad(second, [(0, 0), (0, 0), (0, 2), (0, 0)] + tail).reshape((frame_pad, rows_in, width) + trailing)
    return jnp.pad(first, [(0, 0), (0, 4), (0, 0)] + tail) + jnp.pad(second, [(0, 0), (4, 0), (0, 0)] + tail)

def shift_frames(parts):
    tail = [(0, 0)] * (parts[0].ndim - 1)
    total = jnp.pad(parts[0], [(0, 2)] + tail)
    total = total + jnp.pad(parts[1], [(1, 1)] + tail)
    return total + jnp.pad(parts[2], [(2, 0)] + tail)

def reference(query_tok, key_tok, value_tok, grad_out, head_reach, tile_offset):
    frame_total, row_total, width, packed = query_tok.shape
    heads = head_reach.shape[0]
    head_dim = packed // heads
    tiles = row_total // 4
    inv_root = 1.0 / math.sqrt(head_dim)
    tile_ids = jnp.arange(tiles)[:, None]
    win_rows = jnp.arange(6)[None, :]
    global_row = 4 * tile_ids + win_rows - 1
    offset3 = tile_offset[:, :, None]
    rows_ok = (global_row >= 0) & (global_row < row_total)
    rows_ok = rows_ok[None] & ((win_rows != 0) | (offset3 == -1)) & ((win_rows != 5) | (offset3 == 0))
    rows_ok = jnp.broadcast_to(rows_ok[..., None], rows_ok.shape + (width,)).reshape(frame_total, tiles, 6 * width)
    frame_ids = jnp.arange(frame_total)[:, None] + jnp.arange(3)[None, :] - 1
    frames_ok = (frame_ids >= 0) & (frame_ids < frame_total)
    key_ok = frames_ok[:, None, :, None] & rows_ok[:, :, None, :]
    win_cols = jnp.arange(6 * width) // width
    edge_low = 4 * jnp.arange(tiles) % ROWS_DEV == 0
    edge_high = (4 * jnp.arange(tiles) + 4) % ROWS_DEV == 0
    take_low = (edge_low[:, None] & (win_cols[None, :] == 0))[None, :, :, None, None]
    take_high = (edge_high[:, None] & (win_cols[None, :] == 5))[None, :, :, None, None]

    def one_head(outputs, head):
        grad_q_all, grad_k_all, grad_v_all = outputs
        start = (head * head_dim).astype(jnp.int32)

        def head_slice(array):
            return lax.dynamic_slice_in_dim(array, start, head_dim, 3).astype(jnp.float32)
        query_h = head_slice(query_tok).reshape(frame_total, tiles, 4 * width, head_dim)
        grad_h = head_slice(grad_out).reshape(frame_total, tiles, 4 * width, head_dim)
        pair = jnp.stack([head_slice(key_tok), head_slice(value_tok)], axis=3)
        padded = jnp.pad(pair, ((1, 1), (1, 3), (0, 0), (0, 0), (0, 0)))
        windows = build_windows(padded)
        key_parts = [windows[step:step + frame_total, :, :, 0] for step in range(3)]
        value_parts = [windows[step:step + frame_total, :, :, 1] for step in range(3)]
        heads_ok = (head_reach[head] == 1) | (jnp.arange(3) == 1)
        allowed = key_ok[:, :, None, :, :] & heads_ok[None, None, None, :, None]
        scores = jnp.stack([jnp.einsum('ftqd,ftkd->ftqk', query_h, part) for part in key_parts], axis=3) * inv_root
        scores = jnp.where(allowed, scores, -1e+30)
        top = lax.optimization_barrier(jnp.max(scores, axis=(3, 4), keepdims=True))
        expo = jnp.exp(scores - top)
        probs = expo / lax.optimization_barrier(jnp.sum(expo, axis=(3, 4), keepdims=True))
        weights = probs.astype(jnp.bfloat16).astype(jnp.float32)
        attended = jnp.zeros(query_h.shape, jnp.float32)
        for step in range(3):
            attended = attended + jnp.einsum('ftqk,ftkd->ftqd', weights[:, :, :, step], value_parts[step])
        delta = lax.optimization_barrier(jnp.sum(grad_h * attended, axis=-1))
        dprobs = jnp.stack([jnp.einsum('ftqd,ftkd->ftqk', grad_h, part) for part in value_parts], axis=3)
        dscores = (probs * (dprobs - delta[..., None, None]) * inv_root).astype(jnp.bfloat16).astype(jnp.float32)
        grad_query = jnp.zeros(query_h.shape, jnp.float32)
        pair_parts = []
        for step in range(3):
            grad_query = grad_query + jnp.einsum('ftqk,ftkd->ftqd', dscores[:, :, :, step], key_parts[step])
            key_term = jnp.einsum('ftqk,ftqd->ftkd', dscores[:, :, :, step], query_h)
            value_term = jnp.einsum('ftqk,ftqd->ftkd', weights[:, :, :, step], grad_h)
            pair_parts.append(jnp.stack([key_term, value_term], axis=3))
        spread = shift_frames(pair_parts)
        zeros_f = jnp.zeros_like(spread)
        own_part = fold_windows(jnp.where(take_low | take_high, zeros_f, spread), width)
        low_part = fold_windows(jnp.where(take_low, spread, zeros_f), width)
        high_part = fold_windows(jnp.where(take_high, spread, zeros_f), width)
        own_part = own_part[1:frame_total + 1, 1:row_total + 1]
        low_round = lax.optimization_barrier(low_part[1:frame_total + 1, 1:row_total + 1].astype(jnp.bfloat16))
        high_round = lax.optimization_barrier(high_part[1:frame_total + 1, 1:row_total + 1].astype(jnp.bfloat16))
        pair_total = (own_part + low_round.astype(jnp.float32) + high_round.astype(jnp.float32)).astype(jnp.bfloat16)
        grad_q_head = grad_query.astype(jnp.bfloat16).reshape(frame_total, row_total, width, head_dim)
        grad_q_all = lax.dynamic_update_slice_in_dim(grad_q_all, grad_q_head, start, 3)
        grad_k_all = lax.dynamic_update_slice_in_dim(grad_k_all, pair_total[:, :, :, 0], start, 3)
        grad_v_all = lax.dynamic_update_slice_in_dim(grad_v_all, pair_total[:, :, :, 1], start, 3)
        return ((grad_q_all, grad_k_all, grad_v_all), None)
    empty = jnp.zeros(query_tok.shape, jnp.bfloat16)
    result, _ = lax.scan(one_head, (empty, empty, empty), jnp.arange(heads, dtype=jnp.int32))
    return (result[0], result[1], result[2])
```

```python
import functools
import math

import jax
import jax.numpy as jnp
from jax import lax
from jax.experimental import pallas as pl
from jax.experimental.pallas import tpu as pltpu
from jax.sharding import PartitionSpec as P

F32 = jnp.float32
BF16 = jnp.bfloat16
MASKED = -1e30
TILE_ROWS = 4
NT = (((1,), (1,)), ((), ()))
NN = (((1,), (0,)), ((), ()))
TN = (((0,), (0,)), ((), ()))
QD, ST1, ST2, DQ = range(4)


def dot(a, b, dims):
    return lax.dot_general(a, b, dims, preferred_element_type=F32)


def kernel(
    cfg,
    info,
    penalty,
    offs,
    q_ref,
    k_ref,
    v_ref,
    g_ref,
    oq_ref,
    ok_ref,
    ov_ref,
    qg,
    kv,
    kv_in,
    qd,
    bias,
    e_s,
    dp_s,
    st_mine,
    st_in,
    tot_mine,
    tot_in,
    dq_own,
    dq_out,
    dq_in,
    dk_res,
    dv_res,
    rim_out,
    rim_in,
    kv_send,
    kv_recv,
    f_send,
    f_recv,
    r_send,
    r_recv,
):
    heads, pairs, group, width, tokens, dim, frames, blocks = cfg
    slots = pairs * group
    ext = tokens + 2 * width
    tiles = tokens // (TILE_ROWS * width)
    rows_dev = tokens // width
    inv_root = 1.0 / math.sqrt(dim)
    f = lax.axis_index("frame")
    b = lax.axis_index("row")
    f_has = (f > 0, f < frames - 1)
    b_has = (b > 0, b < blocks - 1)
    f_to = (f - 1, f + 1)
    b_to = (b - 1, b + 1)

    barrier = pltpu.get_barrier_semaphore()
    for d in range(2):

        @pl.when(f_has[d])
        def _():
            pl.semaphore_signal(
                barrier, inc=1, device_id=(f_to[d], b), device_id_type=pl.DeviceIdType.MESH
            )

        @pl.when(b_has[d])
        def _():
            pl.semaphore_signal(
                barrier, inc=1, device_id=(f, b_to[d]), device_id_type=pl.DeviceIdType.MESH
            )

    pl.semaphore_wait(barrier, sum(has.astype(jnp.int32) for has in f_has + b_has))

    def frame_copy(kind, c, d):
        src, dst = {
            QD: lambda: (qd.at[c, 0], qd.at[c, 2 - d]),
            ST1: lambda: (st_mine.at[c, 1 + d], st_in.at[c, 1 - d]),
            ST2: lambda: (tot_mine.at[c], tot_in.at[c, 1 - d]),
            DQ: lambda: (dq_out.at[c, d], dq_in.at[c, 1 - d]),
        }[kind]()
        return pltpu.make_async_remote_copy(
            src_ref=src,
            dst_ref=dst,
            send_sem=f_send.at[kind, c, d],
            recv_sem=f_recv.at[kind, c, 1 - d],
            device_id=(f_to[d], b),
            device_id_type=pl.DeviceIdType.MESH,
        )

    def frame_start(kind, c):
        for d in range(2):

            @pl.when(f_has[d])
            def _():
                frame_copy(kind, c, d).start()

    def frame_arrived(kind, c):
        for d in range(2):

            @pl.when(f_has[d])
            def _():
                frame_copy(kind, c, 1 - d).wait_recv()

    def kv_copy(which, d):
        src = (k_ref, v_ref)[which]
        first = 0 if d == 0 else tokens - width
        return pltpu.make_async_remote_copy(
            src_ref=src.at[pl.ds(first, width)],
            dst_ref=kv_in.at[1 - d, which],
            send_sem=kv_send.at[which, d],
            recv_sem=kv_recv.at[which, 1 - d],
            device_id=(f, b_to[d]),
            device_id_type=pl.DeviceIdType.MESH,
        )

    def rim_copy(first, count, sem, d):
        return pltpu.make_async_remote_copy(
            src_ref=rim_out.at[d, pl.ds(first, count)],
            dst_ref=rim_in.at[1 - d, pl.ds(first, count)],
            send_sem=r_send.at[sem, d],
            recv_sem=r_recv.at[sem, 1 - d],
            device_id=(f, b_to[d]),
            device_id_type=pl.DeviceIdType.MESH,
        )

    def rim_start(first, count, sem):
        for d in range(2):

            @pl.when(b_has[d])
            def _():
                rim_copy(first, count, sem, d).start()

    for d in range(2):

        @pl.when(b_has[d])
        def _():
            for which in range(2):
                kv_copy(which, d).start()

    def lanes(head):
        return pl.ds(pl.multiple_of(head * dim, dim), dim)

    def split_queries(h, _):
        qg[h, 0] = q_ref[:, lanes(h)]
        qg[h, 1] = g_ref[:, lanes(h)]
        return 0

    lax.fori_loop(0, heads, split_queries, 0)

    def gather(c, _):
        for j in range(group):
            qd[c, 0, j] = qg[info[0, c * group + j]]
        frame_start(QD, c)
        return 0

    lax.fori_loop(0, pairs, gather, 0)

    def split_keys(h, _):
        kv[h, 0, pl.ds(width, tokens)] = k_ref[:, lanes(h)]
        kv[h, 1, pl.ds(width, tokens)] = v_ref[:, lanes(h)]
        return 0

    lax.fori_loop(0, heads, split_keys, 0)
    for d in range(2):

        @pl.when(jnp.logical_not(b_has[d]))
        def _():
            kv_in[d] = jnp.zeros(kv_in.shape[1:], BF16)
            rim_in[d] = jnp.zeros(rim_in.shape[1:], BF16)

        if pairs:

            @pl.when(jnp.logical_not(f_has[d]))
            def _():
                qd[:, 1 + d] = jnp.zeros((pairs,) + qd.shape[2:], BF16)
                dq_in[:, d] = jnp.zeros((pairs,) + dq_in.shape[2:], BF16)
                tot_in[:, d] = jnp.zeros((pairs,) + tot_in.shape[2:], F32)
                row = lax.broadcasted_iota(jnp.int32, (pairs,) + st_in.shape[2:], 1)
                st_in[:, d] = jnp.where(row % 4 == 0, MASKED, 0.0).astype(F32)

    key_row = jnp.zeros((ext, tokens), jnp.int32)
    tile = jnp.zeros((ext, tokens), jnp.int32)
    sub = lax.broadcasted_iota(jnp.int32, (ext, tokens), 0)
    lane = lax.broadcasted_iota(jnp.int32, (ext, tokens), 1)
    for r in range(1, rows_dev + 2):
        key_row = key_row + (sub >= r * width).astype(jnp.int32)
    for t in range(1, tiles):
        tile = tile + (lane >= t * TILE_ROWS * width).astype(jnp.int32)
    global_row = b * rows_dev + key_row - 1
    row_ok = (global_row >= 0) & (global_row < blocks * rows_dev)
    for j, frame in enumerate((f, jnp.maximum(f - 1, 0), jnp.minimum(f + 1, frames - 1))):
        off = jnp.zeros((ext, tokens), F32)
        for t in range(tiles):
            off = jnp.where(tile == t, offs[frame, t], off)
        rel = (key_row - 1 - TILE_ROWS * tile).astype(F32) - off
        outside = jnp.maximum(jnp.minimum(jnp.minimum(rel, TILE_ROWS - rel), 0.0), -1.0)
        bias[:, pl.ds(j * tokens, tokens)] = jnp.where(row_ok, -outside * MASKED, MASKED)

    for d in range(2):

        @pl.when(b_has[d])
        def _():
            for which in range(2):
                kv_copy(which, 1 - d).wait_recv()

    def split_rims(h, _):
        for which in range(2):
            kv[h, which, pl.ds(0, width)] = kv_in[0, which, :, lanes(h)]
            kv[h, which, pl.ds(width + tokens, width)] = kv_in[1, which, :, lanes(h)]
        return 0

    lax.fori_loop(0, heads, split_rims, 0)

    def put_key_grads(s, dk, dv):
        dk_res[s] = dk[width : width + tokens]
        dv_res[s] = dv[width : width + tokens]
        rim_out[0, s, 0] = dk[:width].astype(BF16)
        rim_out[0, s, 1] = dv[:width].astype(BF16)
        rim_out[1, s, 0] = dk[width + tokens :].astype(BF16)
        rim_out[1, s, 1] = dv[width + tokens :].astype(BF16)

    def local_heads(i, _):
        for j in range(group):
            s = slots + i * group + j
            head = info[0, s]
            kx, vx = kv[head, 0], kv[head, 1]
            q, g = qg[head, 0], qg[head, 1]
            sc = dot(kx, q, NT) * inv_root + bias[:, pl.ds(0, tokens)]
            e = jnp.exp(sc - jnp.max(sc, axis=0, keepdims=True))
            dp = dot(vx, g, NT)
            inv = 1.0 / jnp.sum(e, axis=0, keepdims=True)
            p = e * inv
            delta = jnp.sum(p * dp, axis=0, keepdims=True)
            ds = (p * (dp - delta) * inv_root).astype(BF16)
            put_key_grads(s, dot(ds, q, NN), dot(p.astype(BF16), g, NN))
            dq_own[s] = dot(ds, kx, TN)
        return 0

    local = heads // group - pairs
    if local:
        lax.fori_loop(0, local, local_heads, 0)
        rim_start(slots, heads - slots, pairs)

    def partial_sums(c):
        frame_arrived(QD, c)
        for j in range(group):
            s = c * group + j
            head = info[0, s]
            absent = [penalty[s] + jnp.where(has, 0.0, MASKED) for has in f_has]
            kx, vx = kv[head, 0], kv[head, 1]
            q = jnp.concatenate([qd[c, part, j, 0] for part in range(3)], axis=0)
            g = jnp.concatenate([qd[c, part, j, 1] for part in range(3)], axis=0)
            sc = dot(kx, q, NT) * inv_root + bias[...]
            top = jnp.max(sc, axis=0, keepdims=True)
            e = jnp.exp(sc - top)
            dp = dot(vx, g, NT)
            e_s[s] = e
            dp_s[s] = dp
            total = jnp.sum(e, axis=0, keepdims=True)
            mixed = jnp.sum(e * dp, axis=0, keepdims=True)
            for part in range(3):
                cut = slice(part * tokens, (part + 1) * tokens)
                m = top[:, cut]
                if part:
                    m = m + absent[part - 1]
                st_mine[c, part, 4 * j : 4 * j + 1] = m
                st_mine[c, part, 4 * j + 1 : 4 * j + 2] = total[:, cut]
                st_mine[c, part, 4 * j + 2 : 4 * j + 3] = mixed[:, cut]
                st_mine[c, part, 4 * j + 3 : 4 * j + 4] = total[:, cut]
        frame_start(ST1, c)

    def combine(c):
        frame_arrived(ST1, c)
        for j in range(group):
            parts = [st_mine.at[c, 0], st_in.at[c, 0], st_in.at[c, 1]]
            m, total, mixed = [
                [p[4 * j + row : 4 * j + row + 1] for p in parts] for row in range(3)
            ]
            top = jnp.maximum(jnp.maximum(m[0], m[1]), m[2])
            scale = [jnp.exp(x - top) for x in m]
            inv = 1.0 / sum(x * y for x, y in zip(scale, total))
            tot_mine[c, 4 * j : 4 * j + 1] = top
            tot_mine[c, 4 * j + 1 : 4 * j + 2] = inv
            tot_mine[c, 4 * j + 2 : 4 * j + 3] = sum(x * y for x, y in zip(scale, mixed)) * inv
            tot_mine[c, 4 * j + 3 : 4 * j + 4] = inv
        frame_start(ST2, c)

    def backward(c):
        frame_arrived(ST2, c)
        for j in range(group):
            s = c * group + j
            kx = kv[info[0, s], 0]
            q = jnp.concatenate([qd[c, part, j, 0] for part in range(3)], axis=0)
            g = jnp.concatenate([qd[c, part, j, 1] for part in range(3)], axis=0)
            whole = [tot_mine.at[c], tot_in.at[c, 0], tot_in.at[c, 1]]
            scale = jnp.concatenate(
                [
                    jnp.exp(st_mine[c, part, 4 * j : 4 * j + 1] - whole[part][4 * j : 4 * j + 1])
                    * whole[part][4 * j + 1 : 4 * j + 2]
                    for part in range(3)
                ],
                axis=1,
            )
            delta = jnp.concatenate(
                [whole[part][4 * j + 2 : 4 * j + 3] for part in range(3)], axis=1
            )
            p = e_s[s] * scale
            ds = (p * (dp_s[s] - delta) * inv_root).astype(BF16)
            put_key_grads(s, dot(ds, q, NN), dot(p.astype(BF16), g, NN))
            dq = dot(ds, kx, TN)
            dq_own[s] = dq[:tokens]
            dq_out[c, 0, j] = dq[tokens : 2 * tokens].astype(BF16)
            dq_out[c, 1, j] = dq[2 * tokens :].astype(BF16)
        frame_start(DQ, c)
        rim_start(c * group, group, c)

    def add_queries(c):
        frame_arrived(DQ, c)
        for j in range(group):
            s = c * group + j
            dq_own[s] = dq_own[s] + (dq_in[c, 0, j].astype(F32) + dq_in[c, 1, j].astype(F32))

    def step(i, _):
        for lag, stage in enumerate((partial_sums, combine, backward, add_queries)):

            @pl.when((i >= lag) & (i < pairs + lag))
            def _():
                stage(i - lag)

        return 0

    if pairs:
        lax.fori_loop(0, pairs + 3, step, 0)

    for d in range(2):

        @pl.when(b_has[d])
        def _():
            for c in range(pairs):
                rim_copy(c * group, group, c, 1 - d).wait_recv()
            if local:
                rim_copy(slots, heads - slots, pairs, 1 - d).wait_recv()

    def assemble(h, _):
        s = info[1, h]
        cols = lanes(h)
        oq_ref[:, cols] = dq_own[s].astype(BF16)
        for which, (res, out) in enumerate(((dk_res, ok_ref), (dv_res, ov_ref))):
            full = res[s]
            first = full[:width] + rim_in[0, s, which].astype(F32)
            last = full[tokens - width :] + rim_in[1, s, which].astype(F32)
            out[:, cols] = jnp.concatenate(
                [first, full[width : tokens - width], last], axis=0
            ).astype(BF16)
        return 0

    lax.fori_loop(0, heads, assemble, 0)

    for d in range(2):

        @pl.when(b_has[d])
        def _():
            for which in range(2):
                kv_copy(which, d).wait_send()
            for c in range(pairs):
                rim_copy(c * group, group, c, d).wait_send()
            if local:
                rim_copy(slots, heads - slots, pairs, d).wait_send()

        if pairs:

            @pl.when(f_has[d])
            def _():
                def sent(c, _):
                    for kind in (QD, ST1, ST2, DQ):
                        frame_copy(kind, c, d).wait_send()
                    return 0

                lax.fori_loop(0, pairs, sent, 0)


def attention(mesh, pairs, group, width, heads, info, penalty, offs, q, k, v, g):
    tokens, packed = q.shape
    dim = packed // heads
    ext = tokens + 2 * width
    frames, blocks = mesh.shape["frame"], mesh.shape["row"]
    slots = pairs * group
    n = max(pairs, 1)
    cfg = (heads, pairs, group, width, tokens, dim, frames, blocks)
    smem = pl.BlockSpec(memory_space=pltpu.SMEM)
    vmem = pl.BlockSpec(memory_space=pltpu.VMEM)
    dma = pltpu.SemaphoreType.DMA
    return pl.pallas_call(
        functools.partial(kernel, cfg),
        out_shape=[jax.ShapeDtypeStruct((tokens, packed), BF16)] * 3,
        in_specs=[smem, smem, smem, vmem, vmem, vmem, vmem],
        out_specs=[vmem, vmem, vmem],
        scratch_shapes=[
            pltpu.VMEM((heads, 2, tokens, dim), BF16),
            pltpu.VMEM((heads, 2, ext, dim), BF16),
            pltpu.VMEM((2, 2, width, packed), BF16),
            pltpu.VMEM((n, 3, group, 2, tokens, dim), BF16),
            pltpu.VMEM((ext, 3 * tokens), F32),
            pltpu.VMEM((max(slots, 1), ext, 3 * tokens), F32),
            pltpu.VMEM((max(slots, 1), ext, 3 * tokens), F32),
            pltpu.VMEM((n, 3, 4 * group, tokens), F32),
            pltpu.VMEM((n, 2, 4 * group, tokens), F32),
            pltpu.VMEM((n, 4 * group, tokens), F32),
            pltpu.VMEM((n, 2, 4 * group, tokens), F32),
            pltpu.VMEM((heads, tokens, dim), F32),
            pltpu.VMEM((n, 2, group, tokens, dim), BF16),
            pltpu.VMEM((n, 2, group, tokens, dim), BF16),
            pltpu.VMEM((heads, tokens, dim), F32),
            pltpu.VMEM((heads, tokens, dim), F32),
            pltpu.VMEM((2, heads, 2, width, dim), BF16),
            pltpu.VMEM((2, heads, 2, width, dim), BF16),
            dma((2, 2)),
            dma((2, 2)),
            dma((4, n, 2)),
            dma((4, n, 2)),
            dma((n + 1, 2)),
            dma((n + 1, 2)),
        ],
        compiler_params=pltpu.CompilerParams(
            collective_id=pairs, has_side_effects=True, vmem_limit_bytes=48 * 2**20
        ),
        cost_estimate=pl.CostEstimate(
            flops=12 * ext * tokens * dim * (heads + 2 * slots),
            bytes_accessed=14 * tokens * packed,
            transcendentals=ext * tokens * (heads + 2 * slots),
        ),
    )(info, penalty, offs, q, k, v, g)


def on_device(mesh, query_tok, key_tok, value_tok, grad_out, head_reach, tile_offset):
    _, rows_dev, width, packed = query_tok.shape
    heads = head_reach.shape[0]
    group = 2 if heads % 2 == 0 else 1
    flat = [x.reshape(rows_dev * width, packed) for x in (query_tok, key_tok, value_tok, grad_out)]
    reach = (head_reach == 1).astype(jnp.int32)
    ids = jnp.arange(heads, dtype=jnp.int32)
    before = jnp.sum(jnp.where(ids[None, :] < ids[:, None], reach[None, :], 0), axis=1)
    count = jnp.sum(reach)
    rank = jnp.where(reach == 1, before, count + ids - before)
    order = jnp.sum(jnp.where(rank[None, :] == ids[:, None], ids[None, :], 0), axis=1)
    info = jnp.stack([order, rank])
    penalty = jnp.where(ids < count, 0.0, MASKED).astype(F32)
    offs = tile_offset.astype(F32)
    all_pairs = heads // group
    sizes = SIZES(all_pairs)
    need = (count + group - 1) // group
    branch = sum((need > size).astype(jnp.int32) for size in sizes[:-1])
    run = [functools.partial(attention, mesh, size, group, width, heads) for size in sizes]
    if len(run) == 1:
        outs = run[0](info, penalty, offs, *flat)
    else:
        outs = lax.switch(branch, run, info, penalty, offs, *flat)
    return tuple(x.reshape(query_tok.shape) for x in outs)


def SIZES(all_pairs):
    return [all_pairs]


def solution(mesh):
    tok = P("frame", "row", None, None)
    return jax.shard_map(
        functools.partial(on_device, mesh),
        mesh=mesh,
        in_specs=(tok, tok, tok, tok, P(), P(None, "row")),
        out_specs=(tok, tok, tok),
        check_vma=False,
    )
```

```python
import functools
import math

import jax
import jax.numpy as jnp
from jax import lax
from jax.experimental import pallas as pl
from jax.experimental.pallas import tpu as pltpu
from jax.sharding import PartitionSpec as P

F32 = jnp.float32
BF16 = jnp.bfloat16
MASKED = -1e30
TILE_ROWS = 4
NT = (((1,), (1,)), ((), ()))
NN = (((1,), (0,)), ((), ()))
TN = (((0,), (0,)), ((), ()))
QD, ST1, ST2, DQ = range(4)


def dot(a, b, dims):
    return lax.dot_general(a, b, dims, preferred_element_type=F32)


def kernel(
    cfg,
    reach,
    offs,
    q_ref,
    k_ref,
    v_ref,
    g_ref,
    oq_ref,
    ok_ref,
    ov_ref,
    rank,
    order,
    qg,
    kv,
    kv_in,
    qd,
    bias,
    e_s,
    dp_s,
    st_mine,
    st_in,
    tot_mine,
    tot_in,
    dq_own,
    dq_out,
    dq_in,
    dk_res,
    dv_res,
    rim_out,
    rim_in,
    loaded,
    kv_send,
    kv_recv,
    f_send,
    f_recv,
    r_send,
    r_recv,
):
    heads, pairs, group, width, tokens, dim, frames, blocks = cfg
    slots = pairs * group
    ext = tokens + 2 * width
    tiles = tokens // (TILE_ROWS * width)
    rows_dev = tokens // width
    inv_root = 1.0 / math.sqrt(dim)
    f = lax.axis_index("frame")
    b = lax.axis_index("row")
    f_has = (f > 0, f < frames - 1)
    b_has = (b > 0, b < blocks - 1)
    f_to = (f - 1, f + 1)
    b_to = (b - 1, b + 1)

    barrier = pltpu.get_barrier_semaphore()
    for d in range(2):

        @pl.when(f_has[d])
        def _():
            pl.semaphore_signal(
                barrier, inc=1, device_id=(f_to[d], b), device_id_type=pl.DeviceIdType.MESH
            )

        @pl.when(b_has[d])
        def _():
            pl.semaphore_signal(
                barrier, inc=1, device_id=(f, b_to[d]), device_id_type=pl.DeviceIdType.MESH
            )

    def lanes(head):
        return pl.ds(pl.multiple_of(head * dim, dim), dim)

    own = pl.ds(width, tokens)

    def load(h, _):
        pltpu.make_async_copy(q_ref.at[:, lanes(h)], qg.at[h, 0], loaded.at[0]).start()
        pltpu.make_async_copy(g_ref.at[:, lanes(h)], qg.at[h, 1], loaded.at[0]).start()
        return 0

    lax.fori_loop(0, heads, load, 0)

    def load_keys(h, _):
        pltpu.make_async_copy(k_ref.at[:, lanes(h)], kv.at[h, 0, own], loaded.at[1]).start()
        pltpu.make_async_copy(v_ref.at[:, lanes(h)], kv.at[h, 1, own], loaded.at[1]).start()
        return 0

    lax.fori_loop(0, heads, load_keys, 0)

    count = sum(reach[h] for h in range(heads))
    seen = 0
    for h in range(heads):
        rank[h] = reach[h] * seen + (1 - reach[h]) * (count + h - seen)
        seen = seen + reach[h]

    def place(s, _):
        head = 0
        for h in range(1, heads):
            apart = rank[h] - s
            head = head + h * jnp.maximum(1 - jnp.maximum(apart, -apart), 0)
        order[s] = head
        return 0

    lax.fori_loop(0, heads, place, 0)

    pl.semaphore_wait(barrier, sum(has.astype(jnp.int32) for has in f_has + b_has))

    def frame_copy(kind, c, d):
        src, dst = {
            QD: lambda: (qd.at[c, 0], qd.at[c, 2 - d]),
            ST1: lambda: (st_mine.at[c, 1 + d], st_in.at[c, 1 - d]),
            ST2: lambda: (tot_mine.at[c], tot_in.at[c, 1 - d]),
            DQ: lambda: (dq_out.at[c, d], dq_in.at[c, 1 - d]),
        }[kind]()
        return pltpu.make_async_remote_copy(
            src_ref=src,
            dst_ref=dst,
            send_sem=f_send.at[kind, c, d],
            recv_sem=f_recv.at[kind, c, 1 - d],
            device_id=(f_to[d], b),
            device_id_type=pl.DeviceIdType.MESH,
        )

    def frame_start(kind, c):
        for d in range(2):

            @pl.when(f_has[d])
            def _():
                frame_copy(kind, c, d).start()

    def frame_arrived(kind, c):
        for d in range(2):

            @pl.when(f_has[d])
            def _():
                frame_copy(kind, c, 1 - d).wait_recv()

    def kv_copy(which, d):
        src = (k_ref, v_ref)[which]
        first = 0 if d == 0 else tokens - width
        return pltpu.make_async_remote_copy(
            src_ref=src.at[pl.ds(first, width)],
            dst_ref=kv_in.at[1 - d, which],
            send_sem=kv_send.at[which, d],
            recv_sem=kv_recv.at[which, 1 - d],
            device_id=(f, b_to[d]),
            device_id_type=pl.DeviceIdType.MESH,
        )

    def rim_copy(first, count, sem, d):
        return pltpu.make_async_remote_copy(
            src_ref=rim_out.at[d, pl.ds(first, count)],
            dst_ref=rim_in.at[1 - d, pl.ds(first, count)],
            send_sem=r_send.at[sem, d],
            recv_sem=r_recv.at[sem, 1 - d],
            device_id=(f, b_to[d]),
            device_id_type=pl.DeviceIdType.MESH,
        )

    def rim_start(first, count, sem):
        for d in range(2):

            @pl.when(b_has[d])
            def _():
                rim_copy(first, count, sem, d).start()

    for d in range(2):

        @pl.when(b_has[d])
        def _():
            for which in range(2):
                kv_copy(which, d).start()

    pltpu.make_async_copy(qg, qg, loaded.at[0]).wait()

    def gather(c, _):
        for j in range(group):
            qd[c, 0, j] = qg[order[c * group + j]]
        frame_start(QD, c)
        return 0

    lax.fori_loop(0, pairs, gather, 0)

    for d in range(2):

        @pl.when(jnp.logical_not(b_has[d]))
        def _():
            kv_in[d] = jnp.zeros(kv_in.shape[1:], BF16)
            rim_in[d] = jnp.zeros(rim_in.shape[1:], BF16)

        if pairs:

            @pl.when(jnp.logical_not(f_has[d]))
            def _():
                qd[:, 1 + d] = jnp.zeros((pairs,) + qd.shape[2:], BF16)
                dq_in[:, d] = jnp.zeros((pairs,) + dq_in.shape[2:], BF16)
                tot_in[:, d] = jnp.zeros((pairs,) + tot_in.shape[2:], F32)
                row = lax.broadcasted_iota(jnp.int32, (pairs,) + st_in.shape[2:], 1)
                st_in[:, d] = jnp.where(row % 4 == 0, MASKED, 0.0).astype(F32)

    key_row = jnp.zeros((ext, tokens), jnp.int32)
    tile = jnp.zeros((ext, tokens), jnp.int32)
    sub = lax.broadcasted_iota(jnp.int32, (ext, tokens), 0)
    lane = lax.broadcasted_iota(jnp.int32, (ext, tokens), 1)
    for r in range(1, rows_dev + 2):
        key_row = key_row + (sub >= r * width).astype(jnp.int32)
    for t in range(1, tiles):
        tile = tile + (lane >= t * TILE_ROWS * width).astype(jnp.int32)
    global_row = b * rows_dev + key_row - 1
    row_ok = (global_row >= 0) & (global_row < blocks * rows_dev)
    for j, frame in enumerate((f, jnp.maximum(f - 1, 0), jnp.minimum(f + 1, frames - 1))):
        off = jnp.zeros((ext, tokens), F32)
        for t in range(tiles):
            off = jnp.where(tile == t, offs[t, frame].astype(F32), off)
        rel = (key_row - 1 - TILE_ROWS * tile).astype(F32) - off
        outside = jnp.maximum(jnp.minimum(jnp.minimum(rel, TILE_ROWS - rel), 0.0), -1.0)
        bias[:, pl.ds(j * tokens, tokens)] = jnp.where(row_ok, -outside * MASKED, MASKED)

    mine = kv.at[:, :, own]
    pltpu.make_async_copy(mine, mine, loaded.at[1]).wait()
    for d in range(2):

        @pl.when(b_has[d])
        def _():
            for which in range(2):
                kv_copy(which, 1 - d).wait_recv()

    def split_rims(h, _):
        for which in range(2):
            kv[h, which, pl.ds(0, width)] = kv_in[0, which, :, lanes(h)]
            kv[h, which, pl.ds(width + tokens, width)] = kv_in[1, which, :, lanes(h)]
        return 0

    lax.fori_loop(0, heads, split_rims, 0)

    def put_key_grads(s, dk, dv):
        dk_res[s] = dk[width : width + tokens]
        dv_res[s] = dv[width : width + tokens]
        rim_out[0, s, 0] = dk[:width].astype(BF16)
        rim_out[0, s, 1] = dv[:width].astype(BF16)
        rim_out[1, s, 0] = dk[width + tokens :].astype(BF16)
        rim_out[1, s, 1] = dv[width + tokens :].astype(BF16)

    def local_heads(i, _):
        for j in range(group):
            s = slots + i * group + j
            head = order[s]
            kx, vx = kv[head, 0], kv[head, 1]
            q, g = qg[head, 0], qg[head, 1]
            sc = dot(kx, q, NT) * inv_root + bias[:, pl.ds(0, tokens)]
            e = jnp.exp(sc - jnp.max(sc, axis=0, keepdims=True))
            dp = dot(vx, g, NT)
            inv = 1.0 / jnp.sum(e, axis=0, keepdims=True)
            p = e * inv
            delta = jnp.sum(p * dp, axis=0, keepdims=True)
            ds = (p * (dp - delta) * inv_root).astype(BF16)
            put_key_grads(s, dot(ds, q, NN), dot(p.astype(BF16), g, NN))
            dq_own[s] = dot(ds, kx, TN)
        return 0

    local = heads // group - pairs
    if local:
        lax.fori_loop(0, local, local_heads, 0)
        rim_start(slots, heads - slots, pairs)

    def partial_sums(c):
        frame_arrived(QD, c)
        for j in range(group):
            s = c * group + j
            head = order[s]
            penalty = jnp.clip(s + 1 - count, 0, 1).astype(F32) * MASKED
            absent = [penalty + jnp.where(has, 0.0, MASKED) for has in f_has]
            kx, vx = kv[head, 0], kv[head, 1]
            q = jnp.concatenate([qd[c, part, j, 0] for part in range(3)], axis=0)
            g = jnp.concatenate([qd[c, part, j, 1] for part in range(3)], axis=0)
            sc = dot(kx, q, NT) * inv_root + bias[...]
            top = jnp.max(sc, axis=0, keepdims=True)
            e = jnp.exp(sc - top)
            dp = dot(vx, g, NT)
            e_s[s] = e
            dp_s[s] = dp
            total = jnp.sum(e, axis=0, keepdims=True)
            mixed = jnp.sum(e * dp, axis=0, keepdims=True)
            for part in range(3):
                cut = slice(part * tokens, (part + 1) * tokens)
                m = top[:, cut]
                if part:
                    m = m + absent[part - 1]
                st_mine[c, part, 4 * j : 4 * j + 1] = m
                st_mine[c, part, 4 * j + 1 : 4 * j + 2] = total[:, cut]
                st_mine[c, part, 4 * j + 2 : 4 * j + 3] = mixed[:, cut]
                st_mine[c, part, 4 * j + 3 : 4 * j + 4] = total[:, cut]
        frame_start(ST1, c)

    def combine(c):
        frame_arrived(ST1, c)
        for j in range(group):
            parts = [st_mine.at[c, 0], st_in.at[c, 0], st_in.at[c, 1]]
            m, total, mixed = [
                [p[4 * j + row : 4 * j + row + 1] for p in parts] for row in range(3)
            ]
            top = jnp.maximum(jnp.maximum(m[0], m[1]), m[2])
            scale = [jnp.exp(x - top) for x in m]
            inv = 1.0 / sum(x * y for x, y in zip(scale, total))
            tot_mine[c, 4 * j : 4 * j + 1] = top
            tot_mine[c, 4 * j + 1 : 4 * j + 2] = inv
            tot_mine[c, 4 * j + 2 : 4 * j + 3] = sum(x * y for x, y in zip(scale, mixed)) * inv
            tot_mine[c, 4 * j + 3 : 4 * j + 4] = inv
        frame_start(ST2, c)

    def backward(c):
        frame_arrived(ST2, c)
        for j in range(group):
            s = c * group + j
            kx = kv[order[s], 0]
            q = jnp.concatenate([qd[c, part, j, 0] for part in range(3)], axis=0)
            g = jnp.concatenate([qd[c, part, j, 1] for part in range(3)], axis=0)
            whole = [tot_mine.at[c], tot_in.at[c, 0], tot_in.at[c, 1]]
            scale = jnp.concatenate(
                [
                    jnp.exp(st_mine[c, part, 4 * j : 4 * j + 1] - whole[part][4 * j : 4 * j + 1])
                    * whole[part][4 * j + 1 : 4 * j + 2]
                    for part in range(3)
                ],
                axis=1,
            )
            delta = jnp.concatenate(
                [whole[part][4 * j + 2 : 4 * j + 3] for part in range(3)], axis=1
            )
            p = e_s[s] * scale
            ds = (p * (dp_s[s] - delta) * inv_root).astype(BF16)
            put_key_grads(s, dot(ds, q, NN), dot(p.astype(BF16), g, NN))
            dq = dot(ds, kx, TN)
            dq_own[s] = dq[:tokens]
            dq_out[c, 0, j] = dq[tokens : 2 * tokens].astype(BF16)
            dq_out[c, 1, j] = dq[2 * tokens :].astype(BF16)
        frame_start(DQ, c)
        rim_start(c * group, group, c)

    def add_queries(c):
        frame_arrived(DQ, c)
        for j in range(group):
            s = c * group + j
            dq_own[s] = dq_own[s] + (dq_in[c, 0, j].astype(F32) + dq_in[c, 1, j].astype(F32))

    def step(i, _):
        for lag, stage in enumerate((partial_sums, combine, backward, add_queries)):

            @pl.when((i >= lag) & (i < pairs + lag))
            def _():
                stage(i - lag)

        return 0

    if pairs:
        lax.fori_loop(0, pairs + 3, step, 0)

    for d in range(2):

        @pl.when(b_has[d])
        def _():
            for c in range(pairs):
                rim_copy(c * group, group, c, 1 - d).wait_recv()
            if local:
                rim_copy(slots, heads - slots, pairs, 1 - d).wait_recv()

    def assemble(h, _):
        s = rank[h]
        cols = lanes(h)
        oq_ref[:, cols] = dq_own[s].astype(BF16)
        for which, (res, out) in enumerate(((dk_res, ok_ref), (dv_res, ov_ref))):
            full = res[s]
            first = full[:width] + rim_in[0, s, which].astype(F32)
            last = full[tokens - width :] + rim_in[1, s, which].astype(F32)
            out[:, cols] = jnp.concatenate(
                [first, full[width : tokens - width], last], axis=0
            ).astype(BF16)
        return 0

    lax.fori_loop(0, heads, assemble, 0)

    for d in range(2):

        @pl.when(b_has[d])
        def _():
            for which in range(2):
                kv_copy(which, d).wait_send()
            for c in range(pairs):
                rim_copy(c * group, group, c, d).wait_send()
            if local:
                rim_copy(slots, heads - slots, pairs, d).wait_send()

        if pairs:

            @pl.when(f_has[d])
            def _():
                def sent(c, _):
                    for kind in (QD, ST1, ST2, DQ):
                        frame_copy(kind, c, d).wait_send()
                    return 0

                lax.fori_loop(0, pairs, sent, 0)


def attention(mesh, pairs, group, width, heads, reach, offs, q, k, v, g):
    tokens, packed = q.shape
    dim = packed // heads
    ext = tokens + 2 * width
    frames, blocks = mesh.shape["frame"], mesh.shape["row"]
    slots = pairs * group
    n = max(pairs, 1)
    cfg = (heads, pairs, group, width, tokens, dim, frames, blocks)
    smem = pl.BlockSpec(memory_space=pltpu.SMEM)
    vmem = pl.BlockSpec(memory_space=pltpu.VMEM)
    hbm = pl.BlockSpec(memory_space=pl.ANY)
    dma = pltpu.SemaphoreType.DMA
    return pl.pallas_call(
        functools.partial(kernel, cfg),
        out_shape=[jax.ShapeDtypeStruct((tokens, packed), BF16)] * 3,
        in_specs=[smem, smem, hbm, hbm, hbm, hbm],
        out_specs=[vmem, vmem, vmem],
        scratch_shapes=[
            pltpu.SMEM((heads,), jnp.int32),
            pltpu.SMEM((heads,), jnp.int32),
            pltpu.VMEM((heads, 2, tokens, dim), BF16),
            pltpu.VMEM((heads, 2, ext, dim), BF16),
            pltpu.VMEM((2, 2, width, packed), BF16),
            pltpu.VMEM((n, 3, group, 2, tokens, dim), BF16),
            pltpu.VMEM((ext, 3 * tokens), F32),
            pltpu.VMEM((max(slots, 1), ext, 3 * tokens), F32),
            pltpu.VMEM((max(slots, 1), ext, 3 * tokens), F32),
            pltpu.VMEM((n, 3, 4 * group, tokens), F32),
            pltpu.VMEM((n, 2, 4 * group, tokens), F32),
            pltpu.VMEM((n, 4 * group, tokens), F32),
            pltpu.VMEM((n, 2, 4 * group, tokens), F32),
            pltpu.VMEM((heads, tokens, dim), F32),
            pltpu.VMEM((n, 2, group, tokens, dim), BF16),
            pltpu.VMEM((n, 2, group, tokens, dim), BF16),
            pltpu.VMEM((heads, tokens, dim), F32),
            pltpu.VMEM((heads, tokens, dim), F32),
            pltpu.VMEM((2, heads, 2, width, dim), BF16),
            pltpu.VMEM((2, heads, 2, width, dim), BF16),
            dma((2,)),
            dma((2, 2)),
            dma((2, 2)),
            dma((4, n, 2)),
            dma((4, n, 2)),
            dma((n + 1, 2)),
            dma((n + 1, 2)),
        ],
        compiler_params=pltpu.CompilerParams(
            collective_id=pairs, has_side_effects=True, vmem_limit_bytes=48 * 2**20
        ),
        cost_estimate=pl.CostEstimate(
            flops=12 * ext * tokens * dim * (heads + 2 * slots),
            bytes_accessed=14 * tokens * packed,
            transcendentals=ext * tokens * (heads + 2 * slots),
        ),
    )(reach, offs, q, k, v, g)


def on_device(mesh, query_tok, key_tok, value_tok, grad_out, head_reach, tile_offset):
    _, rows_dev, width, packed = query_tok.shape
    heads = head_reach.shape[0]
    group = 2 if heads % 2 == 0 else 1
    flat = [x.reshape(rows_dev * width, packed) for x in (query_tok, key_tok, value_tok, grad_out)]
    all_pairs = heads // group
    sizes = SIZES(all_pairs)
    count = jnp.sum(head_reach)
    branch = sum((count > size * group).astype(jnp.int32) for size in sizes[:-1])
    run = [functools.partial(attention, mesh, size, group, width, heads) for size in sizes]
    if len(run) == 1:
        outs = run[0](head_reach, tile_offset.T, *flat)
    else:
        outs = lax.switch(branch, run, head_reach, tile_offset.T, *flat)
    return tuple(x.reshape(query_tok.shape) for x in outs)


def SIZES(all_pairs):
    half = all_pairs // 2
    return sorted({max(half - 1, 0), half, half + 1, min(half + 2, all_pairs), all_pairs})


def solution(mesh):
    tok = P("frame", "row", None, None)
    return jax.shard_map(
        functools.partial(on_device, mesh),
        mesh=mesh,
        in_specs=(tok, tok, tok, tok, P(), P(None, "row")),
        out_specs=(tok, tok, tok),
        check_vma=False,
    )
```

```python
import functools
import math

import jax
import jax.numpy as jnp
from jax import lax
from jax.experimental import pallas as pl
from jax.experimental.pallas import tpu as pltpu
from jax.sharding import PartitionSpec as P

F32 = jnp.float32
BF16 = jnp.bfloat16
MASKED = -1e30
TILE_ROWS = 4
NT = (((1,), (1,)), ((), ()))
NN = (((1,), (0,)), ((), ()))
TN = (((0,), (0,)), ((), ()))
QD, ST1, ST2, DQ = range(4)


def dot(a, b, dims):
    return lax.dot_general(a, b, dims, preferred_element_type=F32)


def kernel(
    cfg,
    reach,
    offs,
    q_ref,
    k_ref,
    v_ref,
    g_ref,
    oq_ref,
    ok_ref,
    ov_ref,
    rank,
    order,
    qg,
    kv,
    kv_in,
    qd,
    bias,
    e_s,
    dp_s,
    st_mine,
    st_in,
    tot_mine,
    tot_in,
    dq_own,
    dq_out,
    dq_in,
    edge,
    rim_out,
    rim_in,
    loaded,
    kv_send,
    kv_recv,
    f_send,
    f_recv,
    r_send,
    r_recv,
):
    heads, pairs, group, width, tokens, dim, frames, blocks = cfg
    slots = pairs * group
    ext = tokens + 2 * width
    tiles = tokens // (TILE_ROWS * width)
    rows_dev = tokens // width
    inv_root = 1.0 / math.sqrt(dim)
    f = lax.axis_index("frame")
    b = lax.axis_index("row")
    f_has = (f > 0, f < frames - 1)
    b_has = (b > 0, b < blocks - 1)
    f_to = (f - 1, f + 1)
    b_to = (b - 1, b + 1)

    barrier = pltpu.get_barrier_semaphore()
    for d in range(2):

        @pl.when(f_has[d])
        def _():
            pl.semaphore_signal(
                barrier, inc=1, device_id=(f_to[d], b), device_id_type=pl.DeviceIdType.MESH
            )

        @pl.when(b_has[d])
        def _():
            pl.semaphore_signal(
                barrier, inc=1, device_id=(f, b_to[d]), device_id_type=pl.DeviceIdType.MESH
            )

    def lanes(head):
        return pl.ds(pl.multiple_of(head * dim, dim), dim)

    own = pl.ds(width, tokens)

    def load(h, _):
        pltpu.make_async_copy(q_ref.at[:, lanes(h)], qg.at[h, 0], loaded.at[0]).start()
        pltpu.make_async_copy(g_ref.at[:, lanes(h)], qg.at[h, 1], loaded.at[0]).start()
        return 0

    lax.fori_loop(0, heads, load, 0)

    def load_keys(h, _):
        pltpu.make_async_copy(k_ref.at[:, lanes(h)], kv.at[h, 0, own], loaded.at[1]).start()
        pltpu.make_async_copy(v_ref.at[:, lanes(h)], kv.at[h, 1, own], loaded.at[1]).start()
        return 0

    lax.fori_loop(0, heads, load_keys, 0)

    count = sum(reach[h] for h in range(heads))
    for h, slot in enumerate(slots_of(reach, heads, count)):
        rank[h] = slot

    def place(s, _):
        head = 0
        for h in range(1, heads):
            apart = rank[h] - s
            head = head + h * jnp.maximum(1 - jnp.maximum(apart, -apart), 0)
        order[s] = head
        return 0

    lax.fori_loop(0, heads, place, 0)

    pl.semaphore_wait(barrier, sum(has.astype(jnp.int32) for has in f_has + b_has))

    def frame_copy(kind, c, d):
        src, dst = {
            QD: lambda: (qd.at[c, 0], qd.at[c, 2 - d]),
            ST1: lambda: (st_mine.at[c, 1 + d], st_in.at[c, 1 - d]),
            ST2: lambda: (tot_mine.at[c], tot_in.at[c, 1 - d]),
            DQ: lambda: (dq_out.at[c, d], dq_in.at[c, 1 - d]),
        }[kind]()
        return pltpu.make_async_remote_copy(
            src_ref=src,
            dst_ref=dst,
            send_sem=f_send.at[kind, c, d],
            recv_sem=f_recv.at[kind, c, 1 - d],
            device_id=(f_to[d], b),
            device_id_type=pl.DeviceIdType.MESH,
        )

    def frame_start(kind, c):
        for d in range(2):

            @pl.when(f_has[d])
            def _():
                frame_copy(kind, c, d).start()

    def frame_arrived(kind, c):
        for d in range(2):

            @pl.when(f_has[d])
            def _():
                frame_copy(kind, c, 1 - d).wait_recv()

    def kv_copy(which, d):
        src = (k_ref, v_ref)[which]
        first = 0 if d == 0 else tokens - width
        return pltpu.make_async_remote_copy(
            src_ref=src.at[pl.ds(first, width)],
            dst_ref=kv_in.at[1 - d, which],
            send_sem=kv_send.at[which, d],
            recv_sem=kv_recv.at[which, 1 - d],
            device_id=(f, b_to[d]),
            device_id_type=pl.DeviceIdType.MESH,
        )

    def rim_copy(first, count, sem, d):
        return pltpu.make_async_remote_copy(
            src_ref=rim_out.at[d, pl.ds(first, count)],
            dst_ref=rim_in.at[1 - d, pl.ds(first, count)],
            send_sem=r_send.at[sem, d],
            recv_sem=r_recv.at[sem, 1 - d],
            device_id=(f, b_to[d]),
            device_id_type=pl.DeviceIdType.MESH,
        )

    def rim_start(first, count, sem):
        for d in range(2):

            @pl.when(b_has[d])
            def _():
                rim_copy(first, count, sem, d).start()

    for d in range(2):

        @pl.when(b_has[d])
        def _():
            for which in range(2):
                kv_copy(which, d).start()

    pltpu.make_async_copy(qg, qg, loaded.at[0]).wait()

    def gather(c, _):
        for j in range(group):
            qd[c, 0, j] = qg[order[c * group + j]]
        frame_start(QD, c)
        return 0

    lax.fori_loop(0, pairs, gather, 0)

    for d in range(2):

        @pl.when(jnp.logical_not(b_has[d]))
        def _():
            kv_in[d] = jnp.zeros(kv_in.shape[1:], BF16)
            rim_in[d] = jnp.zeros(rim_in.shape[1:], BF16)

        if pairs:

            @pl.when(jnp.logical_not(f_has[d]))
            def _():
                qd[:, 1 + d] = jnp.zeros((pairs,) + qd.shape[2:], BF16)
                dq_in[:, d] = jnp.zeros((pairs,) + dq_in.shape[2:], BF16)
                tot_in[:, d] = jnp.zeros((pairs,) + tot_in.shape[2:], F32)
                row = lax.broadcasted_iota(jnp.int32, (pairs,) + st_in.shape[2:], 1)
                st_in[:, d] = jnp.where(row % 4 == 0, MASKED, 0.0).astype(F32)

    key_row = jnp.zeros((ext, tokens), jnp.int32)
    tile = jnp.zeros((ext, tokens), jnp.int32)
    sub = lax.broadcasted_iota(jnp.int32, (ext, tokens), 0)
    lane = lax.broadcasted_iota(jnp.int32, (ext, tokens), 1)
    for r in range(1, rows_dev + 2):
        key_row = key_row + (sub >= r * width).astype(jnp.int32)
    for t in range(1, tiles):
        tile = tile + (lane >= t * TILE_ROWS * width).astype(jnp.int32)
    global_row = b * rows_dev + key_row - 1
    row_ok = (global_row >= 0) & (global_row < blocks * rows_dev)
    for j, frame in enumerate((f, jnp.maximum(f - 1, 0), jnp.minimum(f + 1, frames - 1))):
        off = jnp.zeros((ext, tokens), F32)
        for t in range(tiles):
            off = jnp.where(tile == t, offs[t, frame].astype(F32), off)
        rel = (key_row - 1 - TILE_ROWS * tile).astype(F32) - off
        outside = jnp.maximum(jnp.minimum(jnp.minimum(rel, TILE_ROWS - rel), 0.0), -1.0)
        bias[:, pl.ds(j * tokens, tokens)] = jnp.where(row_ok, -outside * MASKED, MASKED)

    mine = kv.at[:, :, own]
    pltpu.make_async_copy(mine, mine, loaded.at[1]).wait()
    for d in range(2):

        @pl.when(b_has[d])
        def _():
            for which in range(2):
                kv_copy(which, 1 - d).wait_recv()

    def split_rims(h, _):
        for which in range(2):
            kv[h, which, pl.ds(0, width)] = kv_in[0, which, :, lanes(h)]
            kv[h, which, pl.ds(width + tokens, width)] = kv_in[1, which, :, lanes(h)]
        return 0

    lax.fori_loop(0, heads, split_rims, 0)

    def put_key_grads(s, dk, dv):
        for which, (grad, out) in enumerate(((dk, ok_ref), (dv, ov_ref))):
            out[s, width : tokens - width] = grad[2 * width : tokens].astype(BF16)
            edge[s, which, 0] = grad[width : 2 * width]
            edge[s, which, 1] = grad[tokens : tokens + width]
        rim_out[0, s, 0] = dk[:width].astype(BF16)
        rim_out[0, s, 1] = dv[:width].astype(BF16)
        rim_out[1, s, 0] = dk[width + tokens :].astype(BF16)
        rim_out[1, s, 1] = dv[width + tokens :].astype(BF16)

    def local_heads(i, _):
        for j in range(group):
            s = slots + i * group + j
            head = order[s]
            kx, vx = kv[head, 0], kv[head, 1]
            q, g = qg[head, 0], qg[head, 1]
            sc = dot(kx, q, NT) * inv_root + bias[:, pl.ds(0, tokens)]
            e = jnp.exp(sc - jnp.max(sc, axis=0, keepdims=True))
            dp = dot(vx, g, NT)
            inv = 1.0 / jnp.sum(e, axis=0, keepdims=True)
            p = e * inv
            delta = jnp.sum(p * dp, axis=0, keepdims=True)
            ds = (p * (dp - delta) * inv_root).astype(BF16)
            put_key_grads(s, dot(ds, q, NN), dot(p.astype(BF16), g, NN))
            oq_ref[s] = dot(ds, kx, TN).astype(BF16)
        return 0

    local = heads // group - pairs
    if local:
        lax.fori_loop(0, local, local_heads, 0)
        rim_start(slots, heads - slots, pairs)

    def partial_sums(c):
        frame_arrived(QD, c)
        for j in range(group):
            s = c * group + j
            head = order[s]
            penalty = jnp.clip(s + 1 - count, 0, 1).astype(F32) * MASKED
            absent = [penalty + jnp.where(has, 0.0, MASKED) for has in f_has]
            kx, vx = kv[head, 0], kv[head, 1]
            q = jnp.concatenate([qd[c, part, j, 0] for part in range(3)], axis=0)
            g = jnp.concatenate([qd[c, part, j, 1] for part in range(3)], axis=0)
            sc = dot(kx, q, NT) * inv_root + bias[...]
            top = jnp.max(sc, axis=0, keepdims=True)
            e = jnp.exp(sc - top)
            dp = dot(vx, g, NT)
            e_s[s] = e
            dp_s[s] = dp
            total = jnp.sum(e, axis=0, keepdims=True)
            mixed = jnp.sum(e * dp, axis=0, keepdims=True)
            for part in range(3):
                cut = slice(part * tokens, (part + 1) * tokens)
                m = top[:, cut]
                if part:
                    m = m + absent[part - 1]
                st_mine[c, part, 4 * j : 4 * j + 1] = m
                st_mine[c, part, 4 * j + 1 : 4 * j + 2] = total[:, cut]
                st_mine[c, part, 4 * j + 2 : 4 * j + 3] = mixed[:, cut]
                st_mine[c, part, 4 * j + 3 : 4 * j + 4] = total[:, cut]
        frame_start(ST1, c)

    def combine(c):
        frame_arrived(ST1, c)
        for j in range(group):
            parts = [st_mine.at[c, 0], st_in.at[c, 0], st_in.at[c, 1]]
            m, total, mixed = [
                [p[4 * j + row : 4 * j + row + 1] for p in parts] for row in range(3)
            ]
            top = jnp.maximum(jnp.maximum(m[0], m[1]), m[2])
            scale = [jnp.exp(x - top) for x in m]
            inv = 1.0 / sum(x * y for x, y in zip(scale, total))
            tot_mine[c, 4 * j : 4 * j + 1] = top
            tot_mine[c, 4 * j + 1 : 4 * j + 2] = inv
            tot_mine[c, 4 * j + 2 : 4 * j + 3] = sum(x * y for x, y in zip(scale, mixed)) * inv
            tot_mine[c, 4 * j + 3 : 4 * j + 4] = inv
        frame_start(ST2, c)

    def backward(c):
        frame_arrived(ST2, c)
        for j in range(group):
            s = c * group + j
            kx = kv[order[s], 0]
            q = jnp.concatenate([qd[c, part, j, 0] for part in range(3)], axis=0)
            g = jnp.concatenate([qd[c, part, j, 1] for part in range(3)], axis=0)
            whole = [tot_mine.at[c], tot_in.at[c, 0], tot_in.at[c, 1]]
            scale = jnp.concatenate(
                [
                    jnp.exp(st_mine[c, part, 4 * j : 4 * j + 1] - whole[part][4 * j : 4 * j + 1])
                    * whole[part][4 * j + 1 : 4 * j + 2]
                    for part in range(3)
                ],
                axis=1,
            )
            delta = jnp.concatenate(
                [whole[part][4 * j + 2 : 4 * j + 3] for part in range(3)], axis=1
            )
            p = e_s[s] * scale
            ds = (p * (dp_s[s] - delta) * inv_root).astype(BF16)
            put_key_grads(s, dot(ds, q, NN), dot(p.astype(BF16), g, NN))
            dq = dot(ds, kx, TN)
            dq_own[s] = dq[:tokens]
            dq_out[c, 0, j] = dq[tokens : 2 * tokens].astype(BF16)
            dq_out[c, 1, j] = dq[2 * tokens :].astype(BF16)
        frame_start(DQ, c)
        rim_start(c * group, group, c)

    def add_queries(c):
        frame_arrived(DQ, c)
        for j in range(group):
            s = c * group + j
            others = dq_in[c, 0, j].astype(F32) + dq_in[c, 1, j].astype(F32)
            oq_ref[s] = (dq_own[s] + others).astype(BF16)

    def step(i, _):
        for lag, stage in enumerate((partial_sums, combine, backward, add_queries)):

            @pl.when((i >= lag) & (i < pairs + lag))
            def _():
                stage(i - lag)

        return 0

    if pairs:
        lax.fori_loop(0, pairs + 3, step, 0)

    for d in range(2):

        @pl.when(b_has[d])
        def _():
            for c in range(pairs):
                rim_copy(c * group, group, c, 1 - d).wait_recv()
            if local:
                rim_copy(slots, heads - slots, pairs, 1 - d).wait_recv()

    def add_rims(s, _):
        for which, out in enumerate((ok_ref, ov_ref)):
            out[s, :width] = (edge[s, which, 0] + rim_in[0, s, which].astype(F32)).astype(BF16)
            out[s, tokens - width :] = (
                edge[s, which, 1] + rim_in[1, s, which].astype(F32)
            ).astype(BF16)
        return 0

    lax.fori_loop(0, heads, add_rims, 0)

    for d in range(2):

        @pl.when(b_has[d])
        def _():
            for which in range(2):
                kv_copy(which, d).wait_send()
            for c in range(pairs):
                rim_copy(c * group, group, c, d).wait_send()
            if local:
                rim_copy(slots, heads - slots, pairs, d).wait_send()

        if pairs:

            @pl.when(f_has[d])
            def _():
                def sent(c, _):
                    for kind in (QD, ST1, ST2, DQ):
                        frame_copy(kind, c, d).wait_send()
                    return 0

                lax.fori_loop(0, pairs, sent, 0)


def slots_of(reach, heads, count):
    seen = 0
    found = []
    for h in range(heads):
        found.append(reach[h] * seen + (1 - reach[h]) * (count + h - seen))
        seen = seen + reach[h]
    return found


def place_heads(heads, dim, reach, *refs):
    res, out, sem = refs[:3], refs[3:6], refs[6]
    count = sum(reach[h] for h in range(heads))
    for h, slot in enumerate(slots_of(reach, heads, count)):
        for i in range(3):
            pltpu.make_async_copy(
                res[i].at[slot], out[i].at[:, pl.ds(h * dim, dim)], sem.at[i]
            ).start()
    for i in range(3):
        pltpu.make_async_copy(res[i], res[i], sem.at[i]).wait()


def in_head_order(reach, outs):
    heads, tokens, dim = outs[0].shape
    smem = pl.BlockSpec(memory_space=pltpu.SMEM)
    vmem = pl.BlockSpec(memory_space=pltpu.VMEM)
    return pl.pallas_call(
        functools.partial(place_heads, heads, dim),
        out_shape=[jax.ShapeDtypeStruct((tokens, heads * dim), BF16)] * 3,
        in_specs=[smem, vmem, vmem, vmem],
        out_specs=[pl.BlockSpec(memory_space=pl.ANY)] * 3,
        scratch_shapes=[pltpu.SemaphoreType.DMA((3,))],
    )(reach, *outs)


def attention(mesh, pairs, group, width, heads, reach, offs, q, k, v, g):
    tokens, packed = q.shape
    dim = packed // heads
    ext = tokens + 2 * width
    frames, blocks = mesh.shape["frame"], mesh.shape["row"]
    slots = pairs * group
    n = max(pairs, 1)
    cfg = (heads, pairs, group, width, tokens, dim, frames, blocks)
    smem = pl.BlockSpec(memory_space=pltpu.SMEM)
    vmem = pl.BlockSpec(memory_space=pltpu.VMEM)
    hbm = pl.BlockSpec(memory_space=pl.ANY)
    dma = pltpu.SemaphoreType.DMA
    return pl.pallas_call(
        functools.partial(kernel, cfg),
        out_shape=[jax.ShapeDtypeStruct((heads, tokens, dim), BF16)] * 3,
        in_specs=[smem, smem, hbm, hbm, hbm, hbm],
        out_specs=[vmem, vmem, vmem],
        scratch_shapes=[
            pltpu.SMEM((heads,), jnp.int32),
            pltpu.SMEM((heads,), jnp.int32),
            pltpu.VMEM((heads, 2, tokens, dim), BF16),
            pltpu.VMEM((heads, 2, ext, dim), BF16),
            pltpu.VMEM((2, 2, width, packed), BF16),
            pltpu.VMEM((n, 3, group, 2, tokens, dim), BF16),
            pltpu.VMEM((ext, 3 * tokens), F32),
            pltpu.VMEM((max(slots, 1), ext, 3 * tokens), F32),
            pltpu.VMEM((max(slots, 1), ext, 3 * tokens), F32),
            pltpu.VMEM((n, 3, 4 * group, tokens), F32),
            pltpu.VMEM((n, 2, 4 * group, tokens), F32),
            pltpu.VMEM((n, 4 * group, tokens), F32),
            pltpu.VMEM((n, 2, 4 * group, tokens), F32),
            pltpu.VMEM((max(slots, 1), tokens, dim), F32),
            pltpu.VMEM((n, 2, group, tokens, dim), BF16),
            pltpu.VMEM((n, 2, group, tokens, dim), BF16),
            pltpu.VMEM((heads, 2, 2, width, dim), F32),
            pltpu.VMEM((2, heads, 2, width, dim), BF16),
            pltpu.VMEM((2, heads, 2, width, dim), BF16),
            dma((2,)),
            dma((2, 2)),
            dma((2, 2)),
            dma((4, n, 2)),
            dma((4, n, 2)),
            dma((n + 1, 2)),
            dma((n + 1, 2)),
        ],
        compiler_params=pltpu.CompilerParams(
            collective_id=pairs, has_side_effects=True, vmem_limit_bytes=48 * 2**20
        ),
        cost_estimate=pl.CostEstimate(
            flops=12 * ext * tokens * dim * (heads + 2 * slots),
            bytes_accessed=14 * tokens * packed,
            transcendentals=ext * tokens * (heads + 2 * slots),
        ),
    )(reach, offs, q, k, v, g)


def on_device(mesh, query_tok, key_tok, value_tok, grad_out, head_reach, tile_offset):
    _, rows_dev, width, packed = query_tok.shape
    heads = head_reach.shape[0]
    group = 2 if heads % 2 == 0 else 1
    flat = [x.reshape(rows_dev * width, packed) for x in (query_tok, key_tok, value_tok, grad_out)]
    all_pairs = heads // group
    sizes = SIZES(all_pairs)
    branch = jnp.sum(head_reach) + (group - 1 - group * sizes[0])
    if group == 2:
        branch = lax.shift_right_arithmetic(branch, jnp.int32(1))
    run = [functools.partial(attention, mesh, size, group, width, heads) for size in sizes]
    if len(run) == 1:
        outs = run[0](head_reach, tile_offset.T, *flat)
    else:
        outs = lax.switch(branch, run, head_reach, tile_offset.T, *flat)
    return tuple(x.reshape(query_tok.shape) for x in in_head_order(head_reach, outs))


def SIZES(all_pairs):
    return list(range(max(all_pairs // 2 - 1, 0), all_pairs + 1))


def solution(mesh):
    tok = P("frame", "row", None, None)
    return jax.shard_map(
        functools.partial(on_device, mesh),
        mesh=mesh,
        in_specs=(tok, tok, tok, tok, P(), P(None, "row")),
        out_specs=(tok, tok, tok),
        check_vma=False,
    )
```

```python
import functools
import math

import jax
import jax.numpy as jnp
from jax import lax
from jax.experimental import pallas as pl
from jax.experimental.pallas import tpu as pltpu
from jax.sharding import PartitionSpec as P

F32 = jnp.float32
BF16 = jnp.bfloat16
MASKED = -1e30
TILE_ROWS = 4
NT = (((1,), (1,)), ((), ()))
NN = (((1,), (0,)), ((), ()))
TN = (((0,), (0,)), ((), ()))
QD, ST1, ST2, DQ = range(4)


def dot(a, b, dims):
    return lax.dot_general(a, b, dims, preferred_element_type=F32)


def kernel(
    cfg,
    reach,
    offs,
    q_ref,
    k_ref,
    v_ref,
    g_ref,
    oq_ref,
    ok_ref,
    ov_ref,
    rank,
    order,
    qg,
    kv,
    kv_in,
    qd,
    bias,
    e_s,
    dp_s,
    st_mine,
    st_in,
    tot_mine,
    tot_in,
    dq_own,
    dq_out,
    dq_in,
    edge,
    pass_qd,
    pass_dq,
    rim_out,
    rim_in,
    loaded,
    kv_send,
    kv_recv,
    f_send,
    f_recv,
    h1_send,
    h1_recv,
    h2_send,
    h2_recv,
    r_send,
    r_recv,
):
    heads, pairs, group, width, tokens, dim, frames, blocks = cfg
    slots = pairs * group
    ext = tokens + 2 * width
    tiles = tokens // (TILE_ROWS * width)
    rows_dev = tokens // width
    inv_root = 1.0 / math.sqrt(dim)
    f = lax.axis_index("frame")
    b = lax.axis_index("row")
    f_has = (f > 0, f < frames - 1)
    b_has = (b > 0, b < blocks - 1)
    f_to = (f - 1, f + 1)
    b_to = (b - 1, b + 1)

    relaying = pairs > 0 and group == 2 and frames >= 4 and frames % 2 == 0
    mid = frames // 2 - 1
    relays = (0, frames - 1)
    relayed = (f == mid + 1, f == mid)
    is_relay = (f == 0) | (f == frames - 1)
    my_half = (f == frames - 1).astype(jnp.int32)

    barrier = pltpu.get_barrier_semaphore()
    for d in range(2):

        @pl.when(f_has[d])
        def _():
            pl.semaphore_signal(
                barrier, inc=1, device_id=(f_to[d], b), device_id_type=pl.DeviceIdType.MESH
            )

        @pl.when(b_has[d])
        def _():
            pl.semaphore_signal(
                barrier, inc=1, device_id=(f, b_to[d]), device_id_type=pl.DeviceIdType.MESH
            )

    greeted = sum(has.astype(jnp.int32) for has in f_has + b_has)
    if relaying:
        for here, peers in ((is_relay, (mid, mid + 1)), (relayed[0] | relayed[1], relays)):
            greeted = greeted + 2 * here.astype(jnp.int32)

            @pl.when(here)
            def _():
                for peer in peers:
                    pl.semaphore_signal(
                        barrier, inc=1, device_id=(peer, b), device_id_type=pl.DeviceIdType.MESH
                    )

    def lanes(head):
        return pl.ds(pl.multiple_of(head * dim, dim), dim)

    own = pl.ds(width, tokens)

    def load(h, _):
        pltpu.make_async_copy(q_ref.at[:, lanes(h)], qg.at[h, 0], loaded.at[0]).start()
        pltpu.make_async_copy(g_ref.at[:, lanes(h)], qg.at[h, 1], loaded.at[0]).start()
        return 0

    lax.fori_loop(0, heads, load, 0)

    def load_keys(h, _):
        pltpu.make_async_copy(k_ref.at[:, lanes(h)], kv.at[h, 0, own], loaded.at[1]).start()
        pltpu.make_async_copy(v_ref.at[:, lanes(h)], kv.at[h, 1, own], loaded.at[1]).start()
        return 0

    lax.fori_loop(0, heads, load_keys, 0)

    count = sum(reach[h] for h in range(heads))
    for h, slot in enumerate(slots_of(reach, heads, count)):
        rank[h] = slot

    def place(s, _):
        head = 0
        for h in range(1, heads):
            apart = rank[h] - s
            head = head + h * jnp.maximum(1 - jnp.maximum(apart, -apart), 0)
        order[s] = head
        return 0

    lax.fori_loop(0, heads, place, 0)

    pl.semaphore_wait(barrier, greeted)

    def frame_copy(kind, c, d):
        src, dst = {
            QD: lambda: (qd.at[c, 0], qd.at[c, 2 - d]),
            ST1: lambda: (st_mine.at[c, 1 + d], st_in.at[c, 1 - d]),
            ST2: lambda: (tot_mine.at[c], tot_in.at[c, 1 - d]),
            DQ: lambda: (dq_out.at[c, d], dq_in.at[c, 1 - d]),
        }[kind]()
        return pltpu.make_async_remote_copy(
            src_ref=src,
            dst_ref=dst,
            send_sem=f_send.at[kind, c, d],
            recv_sem=f_recv.at[kind, c, 1 - d],
            device_id=(f_to[d], b),
            device_id_type=pl.DeviceIdType.MESH,
        )

    def first_hop(kind, c, d, half):
        src, dst = {
            QD: lambda: (qd.at[c, 0, half], pass_qd.at[c, 1 - d]),
            DQ: lambda: (dq_out.at[c, d, half], pass_dq.at[c, 1 - d]),
        }[kind]()
        return pltpu.make_async_remote_copy(
            src_ref=src,
            dst_ref=dst,
            send_sem=h1_send.at[kind // DQ, c, half],
            recv_sem=h1_recv.at[kind // DQ, c, 1 - d],
            device_id=(relays[half], b),
            device_id_type=pl.DeviceIdType.MESH,
        )

    def second_hop(kind, c, side, half):
        src, dst = {
            QD: lambda: (pass_qd.at[c, side], qd.at[c, 1 + side, half]),
            DQ: lambda: (pass_dq.at[c, side], dq_in.at[c, side, half]),
        }[kind]()
        return pltpu.make_async_remote_copy(
            src_ref=src,
            dst_ref=dst,
            send_sem=h2_send.at[kind // DQ, c, side],
            recv_sem=h2_recv.at[kind // DQ, c, half],
            device_id=(mid + 1 - side, b),
            device_id_type=pl.DeviceIdType.MESH,
        )

    def passes(kind, d):
        if relaying and kind in (QD, DQ):
            return f_has[d] & jnp.logical_not(relayed[d]), relayed[d]
        return f_has[d], None

    def frame_start(kind, c):
        for d in range(2):
            direct, indirect = passes(kind, d)

            @pl.when(direct)
            def _():
                frame_copy(kind, c, d).start()

            if indirect is not None:

                @pl.when(indirect)
                def _():
                    for half in range(2):
                        first_hop(kind, c, d, half).start()

    def frame_arrived(kind, c):
        for d in range(2):
            direct, indirect = passes(kind, d)

            @pl.when(direct)
            def _():
                frame_copy(kind, c, 1 - d).wait_recv()

            if indirect is not None:

                @pl.when(indirect)
                def _():
                    for half in range(2):
                        second_hop(kind, c, d, half).wait_recv()

    def pass_on(kind, c):
        if relaying:

            @pl.when(is_relay & (c >= 0) & (c < pairs))
            def _():
                for side in range(2):
                    first_hop(kind, c, 1 - side, 0).wait_recv()
                    second_hop(kind, c, side, my_half).start()

    def kv_copy(which, d):
        src = (k_ref, v_ref)[which]
        first = 0 if d == 0 else tokens - width
        return pltpu.make_async_remote_copy(
            src_ref=src.at[pl.ds(first, width)],
            dst_ref=kv_in.at[1 - d, which],
            send_sem=kv_send.at[which, d],
            recv_sem=kv_recv.at[which, 1 - d],
            device_id=(f, b_to[d]),
            device_id_type=pl.DeviceIdType.MESH,
        )

    def rim_copy(first, count, sem, d):
        return pltpu.make_async_remote_copy(
            src_ref=rim_out.at[d, pl.ds(first, count)],
            dst_ref=rim_in.at[1 - d, pl.ds(first, count)],
            send_sem=r_send.at[sem, d],
            recv_sem=r_recv.at[sem, 1 - d],
            device_id=(f, b_to[d]),
            device_id_type=pl.DeviceIdType.MESH,
        )

    def rim_start(first, count, sem):
        for d in range(2):

            @pl.when(b_has[d])
            def _():
                rim_copy(first, count, sem, d).start()

    for d in range(2):

        @pl.when(b_has[d])
        def _():
            for which in range(2):
                kv_copy(which, d).start()

    pltpu.make_async_copy(qg, qg, loaded.at[0]).wait()

    def gather(c, _):
        for j in range(group):
            qd[c, 0, j] = qg[order[c * group + j]]
        frame_start(QD, c)
        return 0

    lax.fori_loop(0, pairs, gather, 0)

    for d in range(2):

        @pl.when(jnp.logical_not(b_has[d]))
        def _():
            kv_in[d] = jnp.zeros(kv_in.shape[1:], BF16)
            rim_in[d] = jnp.zeros(rim_in.shape[1:], BF16)

        if pairs:

            @pl.when(jnp.logical_not(f_has[d]))
            def _():
                qd[:, 1 + d] = jnp.zeros((pairs,) + qd.shape[2:], BF16)
                dq_in[:, d] = jnp.zeros((pairs,) + dq_in.shape[2:], BF16)
                tot_in[:, d] = jnp.zeros((pairs,) + tot_in.shape[2:], F32)
                row = lax.broadcasted_iota(jnp.int32, (pairs,) + st_in.shape[2:], 1)
                st_in[:, d] = jnp.where(row % 4 == 0, MASKED, 0.0).astype(F32)

    key_row = jnp.zeros((ext, tokens), jnp.int32)
    tile = jnp.zeros((ext, tokens), jnp.int32)
    sub = lax.broadcasted_iota(jnp.int32, (ext, tokens), 0)
    lane = lax.broadcasted_iota(jnp.int32, (ext, tokens), 1)
    for r in range(1, rows_dev + 2):
        key_row = key_row + (sub >= r * width).astype(jnp.int32)
    for t in range(1, tiles):
        tile = tile + (lane >= t * TILE_ROWS * width).astype(jnp.int32)
    global_row = b * rows_dev + key_row - 1
    row_ok = (global_row >= 0) & (global_row < blocks * rows_dev)
    for j, frame in enumerate((f, jnp.maximum(f - 1, 0), jnp.minimum(f + 1, frames - 1))):
        off = jnp.zeros((ext, tokens), F32)
        for t in range(tiles):
            off = jnp.where(tile == t, offs[t, frame].astype(F32), off)
        rel = (key_row - 1 - TILE_ROWS * tile).astype(F32) - off
        outside = jnp.maximum(jnp.minimum(jnp.minimum(rel, TILE_ROWS - rel), 0.0), -1.0)
        bias[:, pl.ds(j * tokens, tokens)] = jnp.where(row_ok, -outside * MASKED, MASKED)

    mine = kv.at[:, :, own]
    pltpu.make_async_copy(mine, mine, loaded.at[1]).wait()
    for d in range(2):

        @pl.when(b_has[d])
        def _():
            for which in range(2):
                kv_copy(which, 1 - d).wait_recv()

    def split_rims(h, _):
        for which in range(2):
            kv[h, which, pl.ds(0, width)] = kv_in[0, which, :, lanes(h)]
            kv[h, which, pl.ds(width + tokens, width)] = kv_in[1, which, :, lanes(h)]
        return 0

    lax.fori_loop(0, heads, split_rims, 0)

    def put_key_grads(s, dk, dv):
        for which, (grad, out) in enumerate(((dk, ok_ref), (dv, ov_ref))):
            out[s, width : tokens - width] = grad[2 * width : tokens].astype(BF16)
            edge[s, which, 0] = grad[width : 2 * width]
            edge[s, which, 1] = grad[tokens : tokens + width]
        rim_out[0, s, 0] = dk[:width].astype(BF16)
        rim_out[0, s, 1] = dv[:width].astype(BF16)
        rim_out[1, s, 0] = dk[width + tokens :].astype(BF16)
        rim_out[1, s, 1] = dv[width + tokens :].astype(BF16)

    def local_heads(i, _):
        for j in range(group):
            s = slots + i * group + j
            head = order[s]
            kx, vx = kv[head, 0], kv[head, 1]
            q, g = qg[head, 0], qg[head, 1]
            sc = dot(kx, q, NT) * inv_root + bias[:, pl.ds(0, tokens)]
            e = jnp.exp(sc - jnp.max(sc, axis=0, keepdims=True))
            dp = dot(vx, g, NT)
            inv = 1.0 / jnp.sum(e, axis=0, keepdims=True)
            p = e * inv
            delta = jnp.sum(p * dp, axis=0, keepdims=True)
            ds = (p * (dp - delta) * inv_root).astype(BF16)
            put_key_grads(s, dot(ds, q, NN), dot(p.astype(BF16), g, NN))
            oq_ref[s] = dot(ds, kx, TN).astype(BF16)
        pass_on(QD, i)
        return 0

    local = heads // group - pairs
    if local:
        lax.fori_loop(0, local, local_heads, 0)
        rim_start(slots, heads - slots, pairs)

    def partial_sums(c):
        frame_arrived(QD, c)
        for j in range(group):
            s = c * group + j
            head = order[s]
            penalty = jnp.clip(s + 1 - count, 0, 1).astype(F32) * MASKED
            absent = [penalty + jnp.where(has, 0.0, MASKED) for has in f_has]
            kx, vx = kv[head, 0], kv[head, 1]
            q = jnp.concatenate([qd[c, part, j, 0] for part in range(3)], axis=0)
            g = jnp.concatenate([qd[c, part, j, 1] for part in range(3)], axis=0)
            sc = dot(kx, q, NT) * inv_root + bias[...]
            top = jnp.max(sc, axis=0, keepdims=True)
            e = jnp.exp(sc - top)
            dp = dot(vx, g, NT)
            e_s[s] = e
            dp_s[s] = dp
            total = jnp.sum(e, axis=0, keepdims=True)
            mixed = jnp.sum(e * dp, axis=0, keepdims=True)
            for part in range(3):
                cut = slice(part * tokens, (part + 1) * tokens)
                m = top[:, cut]
                if part:
                    m = m + absent[part - 1]
                st_mine[c, part, 4 * j : 4 * j + 1] = m
                st_mine[c, part, 4 * j + 1 : 4 * j + 2] = total[:, cut]
                st_mine[c, part, 4 * j + 2 : 4 * j + 3] = mixed[:, cut]
                st_mine[c, part, 4 * j + 3 : 4 * j + 4] = total[:, cut]
        frame_start(ST1, c)

    def combine(c):
        frame_arrived(ST1, c)
        for j in range(group):
            parts = [st_mine.at[c, 0], st_in.at[c, 0], st_in.at[c, 1]]
            m, total, mixed = [
                [p[4 * j + row : 4 * j + row + 1] for p in parts] for row in range(3)
            ]
            top = jnp.maximum(jnp.maximum(m[0], m[1]), m[2])
            scale = [jnp.exp(x - top) for x in m]
            inv = 1.0 / sum(x * y for x, y in zip(scale, total))
            tot_mine[c, 4 * j : 4 * j + 1] = top
            tot_mine[c, 4 * j + 1 : 4 * j + 2] = inv
            tot_mine[c, 4 * j + 2 : 4 * j + 3] = sum(x * y for x, y in zip(scale, mixed)) * inv
            tot_mine[c, 4 * j + 3 : 4 * j + 4] = inv
        frame_start(ST2, c)

    def backward(c):
        frame_arrived(ST2, c)
        for j in range(group):
            s = c * group + j
            kx = kv[order[s], 0]
            q = jnp.concatenate([qd[c, part, j, 0] for part in range(3)], axis=0)
            g = jnp.concatenate([qd[c, part, j, 1] for part in range(3)], axis=0)
            whole = [tot_mine.at[c], tot_in.at[c, 0], tot_in.at[c, 1]]
            scale = jnp.concatenate(
                [
                    jnp.exp(st_mine[c, part, 4 * j : 4 * j + 1] - whole[part][4 * j : 4 * j + 1])
                    * whole[part][4 * j + 1 : 4 * j + 2]
                    for part in range(3)
                ],
                axis=1,
            )
            delta = jnp.concatenate(
                [whole[part][4 * j + 2 : 4 * j + 3] for part in range(3)], axis=1
            )
            p = e_s[s] * scale
            ds = (p * (dp_s[s] - delta) * inv_root).astype(BF16)
            put_key_grads(s, dot(ds, q, NN), dot(p.astype(BF16), g, NN))
            dq = dot(ds, kx, TN)
            dq_own[s] = dq[:tokens]
            dq_out[c, 0, j] = dq[tokens : 2 * tokens].astype(BF16)
            dq_out[c, 1, j] = dq[2 * tokens :].astype(BF16)
        frame_start(DQ, c)
        rim_start(c * group, group, c)

    def add_queries(c):
        frame_arrived(DQ, c)
        for j in range(group):
            s = c * group + j
            others = dq_in[c, 0, j].astype(F32) + dq_in[c, 1, j].astype(F32)
            oq_ref[s] = (dq_own[s] + others).astype(BF16)

    def step(i, _):
        pass_on(QD, local + i)
        pass_on(DQ, i - 3)
        for lag, stage in enumerate((partial_sums, combine, backward, add_queries)):

            @pl.when((i >= lag) & (i < pairs + lag))
            def _():
                stage(i - lag)

        return 0

    if pairs:
        lax.fori_loop(0, pairs + 3, step, 0)

    for d in range(2):

        @pl.when(b_has[d])
        def _():
            for c in range(pairs):
                rim_copy(c * group, group, c, 1 - d).wait_recv()
            if local:
                rim_copy(slots, heads - slots, pairs, 1 - d).wait_recv()

    def add_rims(s, _):
        for which, out in enumerate((ok_ref, ov_ref)):
            out[s, :width] = (edge[s, which, 0] + rim_in[0, s, which].astype(F32)).astype(BF16)
            out[s, tokens - width :] = (
                edge[s, which, 1] + rim_in[1, s, which].astype(F32)
            ).astype(BF16)
        return 0

    lax.fori_loop(0, heads, add_rims, 0)

    for d in range(2):

        @pl.when(b_has[d])
        def _():
            for which in range(2):
                kv_copy(which, d).wait_send()
            for c in range(pairs):
                rim_copy(c * group, group, c, d).wait_send()
            if local:
                rim_copy(slots, heads - slots, pairs, d).wait_send()

        for kind in (QD, ST1, ST2, DQ) if pairs else ():
            direct, indirect = passes(kind, d)

            @pl.when(direct)
            def _():
                for c in range(pairs):
                    frame_copy(kind, c, d).wait_send()

            if indirect is not None:

                @pl.when(indirect)
                def _():
                    for c in range(pairs):
                        for half in range(2):
                            first_hop(kind, c, d, half).wait_send()

    if relaying:

        @pl.when(is_relay)
        def _():
            for kind in (QD, DQ):
                for c in range(pairs):
                    for side in range(2):
                        second_hop(kind, c, side, my_half).wait_send()


def slots_of(reach, heads, count):
    seen = 0
    found = []
    for h in range(heads):
        found.append(reach[h] * seen + (1 - reach[h]) * (count + h - seen))
        seen = seen + reach[h]
    return found


def place_heads(heads, dim, reach, *refs):
    res, out, sem = refs[:3], refs[3:6], refs[6]
    count = sum(reach[h] for h in range(heads))
    for h, slot in enumerate(slots_of(reach, heads, count)):
        for i in range(3):
            pltpu.make_async_copy(
                res[i].at[slot], out[i].at[:, pl.ds(h * dim, dim)], sem.at[i]
            ).start()
    for i in range(3):
        pltpu.make_async_copy(res[i], res[i], sem.at[i]).wait()


def in_head_order(reach, outs):
    heads, tokens, dim = outs[0].shape
    smem = pl.BlockSpec(memory_space=pltpu.SMEM)
    vmem = pl.BlockSpec(memory_space=pltpu.VMEM)
    return pl.pallas_call(
        functools.partial(place_heads, heads, dim),
        out_shape=[jax.ShapeDtypeStruct((tokens, heads * dim), BF16)] * 3,
        in_specs=[smem, vmem, vmem, vmem],
        out_specs=[pl.BlockSpec(memory_space=pl.ANY)] * 3,
        scratch_shapes=[pltpu.SemaphoreType.DMA((3,))],
    )(reach, *outs)


def attention(mesh, pairs, group, width, heads, reach, offs, q, k, v, g):
    tokens, packed = q.shape
    dim = packed // heads
    ext = tokens + 2 * width
    frames, blocks = mesh.shape["frame"], mesh.shape["row"]
    slots = pairs * group
    n = max(pairs, 1)
    cfg = (heads, pairs, group, width, tokens, dim, frames, blocks)
    smem = pl.BlockSpec(memory_space=pltpu.SMEM)
    vmem = pl.BlockSpec(memory_space=pltpu.VMEM)
    hbm = pl.BlockSpec(memory_space=pl.ANY)
    dma = pltpu.SemaphoreType.DMA
    return pl.pallas_call(
        functools.partial(kernel, cfg),
        out_shape=[jax.ShapeDtypeStruct((heads, tokens, dim), BF16)] * 3,
        in_specs=[smem, smem, hbm, hbm, hbm, hbm],
        out_specs=[vmem, vmem, vmem],
        scratch_shapes=[
            pltpu.SMEM((heads,), jnp.int32),
            pltpu.SMEM((heads,), jnp.int32),
            pltpu.VMEM((heads, 2, tokens, dim), BF16),
            pltpu.VMEM((heads, 2, ext, dim), BF16),
            pltpu.VMEM((2, 2, width, packed), BF16),
            pltpu.VMEM((n, 3, group, 2, tokens, dim), BF16),
            pltpu.VMEM((ext, 3 * tokens), F32),
            pltpu.VMEM((max(slots, 1), ext, 3 * tokens), F32),
            pltpu.VMEM((max(slots, 1), ext, 3 * tokens), F32),
            pltpu.VMEM((n, 3, 4 * group, tokens), F32),
            pltpu.VMEM((n, 2, 4 * group, tokens), F32),
            pltpu.VMEM((n, 4 * group, tokens), F32),
            pltpu.VMEM((n, 2, 4 * group, tokens), F32),
            pltpu.VMEM((max(slots, 1), tokens, dim), F32),
            pltpu.VMEM((n, 2, group, tokens, dim), BF16),
            pltpu.VMEM((n, 2, group, tokens, dim), BF16),
            pltpu.VMEM((heads, 2, 2, width, dim), F32),
            pltpu.VMEM((n, 2, 2, tokens, dim), BF16),
            pltpu.VMEM((n, 2, tokens, dim), BF16),
            pltpu.VMEM((2, heads, 2, width, dim), BF16),
            pltpu.VMEM((2, heads, 2, width, dim), BF16),
            dma((2,)),
            dma((2, 2)),
            dma((2, 2)),
            dma((4, n, 2)),
            dma((4, n, 2)),
            dma((2, n, 2)),
            dma((2, n, 2)),
            dma((2, n, 2)),
            dma((2, n, 2)),
            dma((n + 1, 2)),
            dma((n + 1, 2)),
        ],
        compiler_params=pltpu.CompilerParams(
            collective_id=pairs, has_side_effects=True, vmem_limit_bytes=48 * 2**20
        ),
        cost_estimate=pl.CostEstimate(
            flops=12 * ext * tokens * dim * (heads + 2 * slots),
            bytes_accessed=14 * tokens * packed,
            transcendentals=ext * tokens * (heads + 2 * slots),
        ),
    )(reach, offs, q, k, v, g)


def on_device(mesh, query_tok, key_tok, value_tok, grad_out, head_reach, tile_offset):
    _, rows_dev, width, packed = query_tok.shape
    heads = head_reach.shape[0]
    group = 2 if heads % 2 == 0 else 1
    flat = [x.reshape(rows_dev * width, packed) for x in (query_tok, key_tok, value_tok, grad_out)]
    all_pairs = heads // group
    sizes = SIZES(all_pairs)
    branch = jnp.sum(head_reach) + (group - 1 - group * sizes[0])
    if group == 2:
        branch = lax.shift_right_arithmetic(branch, jnp.int32(1))
    run = [functools.partial(attention, mesh, size, group, width, heads) for size in sizes]
    if len(run) == 1:
        outs = run[0](head_reach, tile_offset.T, *flat)
    else:
        outs = lax.switch(branch, run, head_reach, tile_offset.T, *flat)
    return tuple(x.reshape(query_tok.shape) for x in in_head_order(head_reach, outs))


def SIZES(all_pairs):
    return list(range(max(all_pairs // 2 - 1, 0), all_pairs + 1))


def solution(mesh):
    tok = P("frame", "row", None, None)
    return jax.shard_map(
        functools.partial(on_device, mesh),
        mesh=mesh,
        in_specs=(tok, tok, tok, tok, P(), P(None, "row")),
        out_specs=(tok, tok, tok),
        check_vma=False,
    )
```

```python
import functools
import math

import jax
import jax.numpy as jnp
from jax import lax
from jax.experimental import pallas as pl
from jax.experimental.pallas import tpu as pltpu
from jax.sharding import PartitionSpec as P

F32 = jnp.float32
BF16 = jnp.bfloat16
MASKED = -1e30
TILE_ROWS = 4
NT = (((1,), (1,)), ((), ()))
NN = (((1,), (0,)), ((), ()))
TN = (((0,), (0,)), ((), ()))
QD, ST1, ST2, DQ = range(4)


def dot(a, b, dims):
    return lax.dot_general(a, b, dims, preferred_element_type=F32)


def kernel(
    cfg,
    reach,
    offs,
    q_ref,
    k_ref,
    v_ref,
    g_ref,
    oq_ref,
    ok_ref,
    ov_ref,
    rank,
    order,
    qg,
    kv,
    kv_in,
    qd,
    bias,
    e_s,
    dp_s,
    st_mine,
    st_in,
    tot_mine,
    tot_in,
    dq_own,
    dq_out,
    dq_in,
    edge,
    rim_out,
    rim_in,
    loaded,
    kv_send,
    kv_recv,
    f_send,
    f_recv,
    r_send,
    r_recv,
):
    heads, pairs, group, width, tokens, dim, frames, blocks = cfg
    slots = pairs * group
    ext = tokens + 2 * width
    tiles = tokens // (TILE_ROWS * width)
    rows_dev = tokens // width
    inv_root = 1.0 / math.sqrt(dim)
    f = lax.axis_index("frame")
    b = lax.axis_index("row")
    f_has = (f > 0, f < frames - 1)
    b_has = (b > 0, b < blocks - 1)
    f_to = (f - 1, f + 1)
    b_to = (b - 1, b + 1)

    barrier = pltpu.get_barrier_semaphore()
    for d in range(2):

        @pl.when(f_has[d])
        def _():
            pl.semaphore_signal(
                barrier, inc=1, device_id=(f_to[d], b), device_id_type=pl.DeviceIdType.MESH
            )

        @pl.when(b_has[d])
        def _():
            pl.semaphore_signal(
                barrier, inc=1, device_id=(f, b_to[d]), device_id_type=pl.DeviceIdType.MESH
            )

    def lanes(head):
        return pl.ds(pl.multiple_of(head * dim, dim), dim)

    own = pl.ds(width, tokens)

    def load(h, _):
        pltpu.make_async_copy(q_ref.at[:, lanes(h)], qg.at[h, 0], loaded.at[0]).start()
        pltpu.make_async_copy(g_ref.at[:, lanes(h)], qg.at[h, 1], loaded.at[0]).start()
        return 0

    lax.fori_loop(0, heads, load, 0)

    def load_keys(h, _):
        pltpu.make_async_copy(k_ref.at[:, lanes(h)], kv.at[h, 0, own], loaded.at[1]).start()
        pltpu.make_async_copy(v_ref.at[:, lanes(h)], kv.at[h, 1, own], loaded.at[1]).start()
        return 0

    lax.fori_loop(0, heads, load_keys, 0)

    count = sum(reach[h] for h in range(heads))
    for h, slot in enumerate(slots_of(reach, heads, count)):
        rank[h] = slot

    def place(s, _):
        head = 0
        for h in range(1, heads):
            apart = rank[h] - s
            head = head + h * jnp.maximum(1 - jnp.maximum(apart, -apart), 0)
        order[s] = head
        return 0

    lax.fori_loop(0, heads, place, 0)

    pl.semaphore_wait(barrier, sum(has.astype(jnp.int32) for has in f_has + b_has))

    def frame_copy(kind, c, d):
        src, dst = {
            QD: lambda: (qd.at[c, 0], qd.at[c, 2 - d]),
            ST1: lambda: (st_mine.at[c, 1 + d], st_in.at[c, 1 - d]),
            ST2: lambda: (tot_mine.at[c], tot_in.at[c, 1 - d]),
            DQ: lambda: (dq_out.at[c, d], dq_in.at[c, 1 - d]),
        }[kind]()
        return pltpu.make_async_remote_copy(
            src_ref=src,
            dst_ref=dst,
            send_sem=f_send.at[kind, c, d],
            recv_sem=f_recv.at[kind, c, 1 - d],
            device_id=(f_to[d], b),
            device_id_type=pl.DeviceIdType.MESH,
        )

    def frame_start(kind, c):
        for d in range(2):

            @pl.when(f_has[d])
            def _():
                frame_copy(kind, c, d).start()

    def frame_arrived(kind, c):
        for d in range(2):

            @pl.when(f_has[d])
            def _():
                frame_copy(kind, c, 1 - d).wait_recv()

    def kv_copy(which, d):
        src = (k_ref, v_ref)[which]
        first = 0 if d == 0 else tokens - width
        return pltpu.make_async_remote_copy(
            src_ref=src.at[pl.ds(first, width)],
            dst_ref=kv_in.at[1 - d, which],
            send_sem=kv_send.at[which, d],
            recv_sem=kv_recv.at[which, 1 - d],
            device_id=(f, b_to[d]),
            device_id_type=pl.DeviceIdType.MESH,
        )

    def rim_copy(first, count, sem, d):
        return pltpu.make_async_remote_copy(
            src_ref=rim_out.at[d, pl.ds(first, count)],
            dst_ref=rim_in.at[1 - d, pl.ds(first, count)],
            send_sem=r_send.at[sem, d],
            recv_sem=r_recv.at[sem, 1 - d],
            device_id=(f, b_to[d]),
            device_id_type=pl.DeviceIdType.MESH,
        )

    def rim_start(first, count, sem):
        for d in range(2):

            @pl.when(b_has[d])
            def _():
                rim_copy(first, count, sem, d).start()

    for d in range(2):

        @pl.when(b_has[d])
        def _():
            for which in range(2):
                kv_copy(which, d).start()

    pltpu.make_async_copy(qg, qg, loaded.at[0]).wait()

    def gather(c, _):
        for j in range(group):
            qd[c, 0, j] = qg[order[c * group + j]]
        frame_start(QD, c)
        return 0

    lax.fori_loop(0, pairs, gather, 0)

    for d in range(2):

        @pl.when(jnp.logical_not(b_has[d]))
        def _():
            kv_in[d] = jnp.zeros(kv_in.shape[1:], BF16)
            rim_in[d] = jnp.zeros(rim_in.shape[1:], BF16)

        if pairs:

            @pl.when(jnp.logical_not(f_has[d]))
            def _():
                qd[:, 1 + d] = jnp.zeros((pairs,) + qd.shape[2:], BF16)
                dq_in[:, d] = jnp.zeros((pairs,) + dq_in.shape[2:], BF16)
                tot_in[:, d] = jnp.zeros((pairs,) + tot_in.shape[2:], F32)
                row = lax.broadcasted_iota(jnp.int32, (pairs,) + st_in.shape[2:], 1)
                st_in[:, d] = jnp.where(row % 4 == 0, MASKED, 0.0).astype(F32)

    key_row = jnp.zeros((ext, tokens), jnp.int32)
    tile = jnp.zeros((ext, tokens), jnp.int32)
    sub = lax.broadcasted_iota(jnp.int32, (ext, tokens), 0)
    lane = lax.broadcasted_iota(jnp.int32, (ext, tokens), 1)
    for r in range(1, rows_dev + 2):
        key_row = key_row + (sub >= r * width).astype(jnp.int32)
    for t in range(1, tiles):
        tile = tile + (lane >= t * TILE_ROWS * width).astype(jnp.int32)
    global_row = b * rows_dev + key_row - 1
    row_ok = (global_row >= 0) & (global_row < blocks * rows_dev)
    for j, frame in enumerate((f, jnp.maximum(f - 1, 0), jnp.minimum(f + 1, frames - 1))):
        off = jnp.zeros((ext, tokens), F32)
        for t in range(tiles):
            off = jnp.where(tile == t, offs[t, frame].astype(F32), off)
        rel = (key_row - 1 - TILE_ROWS * tile).astype(F32) - off
        outside = jnp.maximum(jnp.minimum(jnp.minimum(rel, TILE_ROWS - rel), 0.0), -1.0)
        bias[:, pl.ds(j * tokens, tokens)] = jnp.where(row_ok, -outside * MASKED, MASKED)

    mine = kv.at[:, :, own]
    pltpu.make_async_copy(mine, mine, loaded.at[1]).wait()
    for d in range(2):

        @pl.when(b_has[d])
        def _():
            for which in range(2):
                kv_copy(which, 1 - d).wait_recv()

    def split_rims(h, _):
        for which in range(2):
            kv[h, which, pl.ds(0, width)] = kv_in[0, which, :, lanes(h)]
            kv[h, which, pl.ds(width + tokens, width)] = kv_in[1, which, :, lanes(h)]
        return 0

    lax.fori_loop(0, heads, split_rims, 0)

    def put_key_grads(s, dk, dv):
        for which, (grad, out) in enumerate(((dk, ok_ref), (dv, ov_ref))):
            out[s, width : tokens - width] = grad[2 * width : tokens].astype(BF16)
            edge[s, which, 0] = grad[width : 2 * width]
            edge[s, which, 1] = grad[tokens : tokens + width]
        rim_out[0, s, 0] = dk[:width].astype(BF16)
        rim_out[0, s, 1] = dv[:width].astype(BF16)
        rim_out[1, s, 0] = dk[width + tokens :].astype(BF16)
        rim_out[1, s, 1] = dv[width + tokens :].astype(BF16)

    def local_heads(i, _):
        for j in range(group):
            s = slots + i * group + j
            head = order[s]
            kx, vx = kv[head, 0], kv[head, 1]
            q, g = qg[head, 0], qg[head, 1]
            sc = dot(kx, q, NT) * inv_root + bias[:, pl.ds(0, tokens)]
            e = jnp.exp(sc - jnp.max(sc, axis=0, keepdims=True))
            dp = dot(vx, g, NT)
            inv = 1.0 / jnp.sum(e, axis=0, keepdims=True)
            p = e * inv
            delta = jnp.sum(p * dp, axis=0, keepdims=True)
            ds = (p * (dp - delta) * inv_root).astype(BF16)
            put_key_grads(s, dot(ds, q, NN), dot(p.astype(BF16), g, NN))
            oq_ref[s] = dot(ds, kx, TN).astype(BF16)
        return 0

    local = heads // group - pairs
    if local:
        lax.fori_loop(0, local, local_heads, 0)
        rim_start(slots, heads - slots, pairs)

    def partial_sums(c):
        frame_arrived(QD, c)
        for j in range(group):
            s = c * group + j
            head = order[s]
            penalty = jnp.clip(s + 1 - count, 0, 1).astype(F32) * MASKED
            absent = [penalty + jnp.where(has, 0.0, MASKED) for has in f_has]
            kx, vx = kv[head, 0], kv[head, 1]
            for part in range(3):
                cut = pl.ds(part * tokens, tokens)
                sc = dot(kx, qd[c, part, j, 0], NT) * inv_root + bias[:, cut]
                top = jnp.max(sc, axis=0, keepdims=True)
                e = jnp.exp(sc - top)
                dp = dot(vx, qd[c, part, j, 1], NT)
                e_s[s, part] = e
                dp_s[s, part] = dp
                total = jnp.sum(e, axis=0, keepdims=True)
                if part:
                    top = top + absent[part - 1]
                st_mine[c, part, 4 * j : 4 * j + 1] = top
                st_mine[c, part, 4 * j + 1 : 4 * j + 2] = total
                st_mine[c, part, 4 * j + 2 : 4 * j + 3] = jnp.sum(e * dp, axis=0, keepdims=True)
                st_mine[c, part, 4 * j + 3 : 4 * j + 4] = total
        frame_start(ST1, c)

    def combine(c):
        frame_arrived(ST1, c)
        for j in range(group):
            parts = [st_mine.at[c, 0], st_in.at[c, 0], st_in.at[c, 1]]
            m, total, mixed = [
                [p[4 * j + row : 4 * j + row + 1] for p in parts] for row in range(3)
            ]
            top = jnp.maximum(jnp.maximum(m[0], m[1]), m[2])
            scale = [jnp.exp(x - top) for x in m]
            inv = 1.0 / sum(x * y for x, y in zip(scale, total))
            tot_mine[c, 4 * j : 4 * j + 1] = top
            tot_mine[c, 4 * j + 1 : 4 * j + 2] = inv
            tot_mine[c, 4 * j + 2 : 4 * j + 3] = sum(x * y for x, y in zip(scale, mixed)) * inv
            tot_mine[c, 4 * j + 3 : 4 * j + 4] = inv
        frame_start(ST2, c)

    def backward(c):
        frame_arrived(ST2, c)
        for j in range(group):
            s = c * group + j
            kx = kv[order[s], 0]
            whole = [tot_mine.at[c], tot_in.at[c, 0], tot_in.at[c, 1]]
            dk = dv = 0.0
            for part in range(3):
                top, inv, delta = [
                    whole[part][4 * j + row : 4 * j + row + 1] for row in range(3)
                ]
                p = e_s[s, part] * (jnp.exp(st_mine[c, part, 4 * j : 4 * j + 1] - top) * inv)
                ds = (p * (dp_s[s, part] - delta) * inv_root).astype(BF16)
                dv = dv + dot(p.astype(BF16), qd[c, part, j, 1], NN)
                dk = dk + dot(ds, qd[c, part, j, 0], NN)
                dq = dot(ds, kx, TN)
                if part:
                    dq_out[c, part - 1, j] = dq.astype(BF16)
                else:
                    dq_own[s] = dq
            put_key_grads(s, dk, dv)
        frame_start(DQ, c)
        rim_start(c * group, group, c)

    def add_queries(c):
        frame_arrived(DQ, c)
        for j in range(group):
            s = c * group + j
            others = dq_in[c, 0, j].astype(F32) + dq_in[c, 1, j].astype(F32)
            oq_ref[s] = (dq_own[s] + others).astype(BF16)

    def step(i, _):
        for lag, stage in enumerate((partial_sums, combine, backward, add_queries)):

            @pl.when((i >= lag) & (i < pairs + lag))
            def _():
                stage(i - lag)

        return 0

    if pairs:
        lax.fori_loop(0, pairs + 3, step, 0)

    for d in range(2):

        @pl.when(b_has[d])
        def _():
            for c in range(pairs):
                rim_copy(c * group, group, c, 1 - d).wait_recv()
            if local:
                rim_copy(slots, heads - slots, pairs, 1 - d).wait_recv()

    def add_rims(s, _):
        for which, out in enumerate((ok_ref, ov_ref)):
            out[s, :width] = (edge[s, which, 0] + rim_in[0, s, which].astype(F32)).astype(BF16)
            out[s, tokens - width :] = (
                edge[s, which, 1] + rim_in[1, s, which].astype(F32)
            ).astype(BF16)
        return 0

    lax.fori_loop(0, heads, add_rims, 0)

    for d in range(2):

        @pl.when(b_has[d])
        def _():
            for which in range(2):
                kv_copy(which, d).wait_send()
            for c in range(pairs):
                rim_copy(c * group, group, c, d).wait_send()
            if local:
                rim_copy(slots, heads - slots, pairs, d).wait_send()

        if pairs:

            @pl.when(f_has[d])
            def _():
                def sent(c, _):
                    for kind in (QD, ST1, ST2, DQ):
                        frame_copy(kind, c, d).wait_send()
                    return 0

                lax.fori_loop(0, pairs, sent, 0)


def slots_of(reach, heads, count):
    seen = 0
    found = []
    for h in range(heads):
        found.append(reach[h] * seen + (1 - reach[h]) * (count + h - seen))
        seen = seen + reach[h]
    return found


def place_heads(heads, dim, reach, *refs):
    res, out, sem = refs[:3], refs[3:6], refs[6]
    count = sum(reach[h] for h in range(heads))
    for h, slot in enumerate(slots_of(reach, heads, count)):
        for i in range(3):
            pltpu.make_async_copy(
                res[i].at[slot], out[i].at[:, pl.ds(h * dim, dim)], sem.at[i]
            ).start()
    for i in range(3):
        pltpu.make_async_copy(res[i], res[i], sem.at[i]).wait()


def in_head_order(reach, outs):
    heads, tokens, dim = outs[0].shape
    smem = pl.BlockSpec(memory_space=pltpu.SMEM)
    vmem = pl.BlockSpec(memory_space=pltpu.VMEM)
    return pl.pallas_call(
        functools.partial(place_heads, heads, dim),
        out_shape=[jax.ShapeDtypeStruct((tokens, heads * dim), BF16)] * 3,
        in_specs=[smem, vmem, vmem, vmem],
        out_specs=[pl.BlockSpec(memory_space=pl.ANY)] * 3,
        scratch_shapes=[pltpu.SemaphoreType.DMA((3,))],
    )(reach, *outs)


def attention(mesh, pairs, group, width, heads, reach, offs, q, k, v, g):
    tokens, packed = q.shape
    dim = packed // heads
    ext = tokens + 2 * width
    frames, blocks = mesh.shape["frame"], mesh.shape["row"]
    slots = pairs * group
    n = max(pairs, 1)
    cfg = (heads, pairs, group, width, tokens, dim, frames, blocks)
    smem = pl.BlockSpec(memory_space=pltpu.SMEM)
    vmem = pl.BlockSpec(memory_space=pltpu.VMEM)
    hbm = pl.BlockSpec(memory_space=pl.ANY)
    dma = pltpu.SemaphoreType.DMA
    return pl.pallas_call(
        functools.partial(kernel, cfg),
        out_shape=[jax.ShapeDtypeStruct((heads, tokens, dim), BF16)] * 3,
        in_specs=[smem, smem, hbm, hbm, hbm, hbm],
        out_specs=[vmem, vmem, vmem],
        scratch_shapes=[
            pltpu.SMEM((heads,), jnp.int32),
            pltpu.SMEM((heads,), jnp.int32),
            pltpu.VMEM((heads, 2, tokens, dim), BF16),
            pltpu.VMEM((heads, 2, ext, dim), BF16),
            pltpu.VMEM((2, 2, width, packed), BF16),
            pltpu.VMEM((n, 3, group, 2, tokens, dim), BF16),
            pltpu.VMEM((ext, 3 * tokens), F32),
            pltpu.VMEM((max(slots, 1), 3, ext, tokens), F32),
            pltpu.VMEM((max(slots, 1), 3, ext, tokens), F32),
            pltpu.VMEM((n, 3, 4 * group, tokens), F32),
            pltpu.VMEM((n, 2, 4 * group, tokens), F32),
            pltpu.VMEM((n, 4 * group, tokens), F32),
            pltpu.VMEM((n, 2, 4 * group, tokens), F32),
            pltpu.VMEM((max(slots, 1), tokens, dim), F32),
            pltpu.VMEM((n, 2, group, tokens, dim), BF16),
            pltpu.VMEM((n, 2, group, tokens, dim), BF16),
            pltpu.VMEM((heads, 2, 2, width, dim), F32),
            pltpu.VMEM((2, heads, 2, width, dim), BF16),
            pltpu.VMEM((2, heads, 2, width, dim), BF16),
            dma((2,)),
            dma((2, 2)),
            dma((2, 2)),
            dma((4, n, 2)),
            dma((4, n, 2)),
            dma((n + 1, 2)),
            dma((n + 1, 2)),
        ],
        compiler_params=pltpu.CompilerParams(
            collective_id=pairs, has_side_effects=True, vmem_limit_bytes=48 * 2**20
        ),
        cost_estimate=pl.CostEstimate(
            flops=12 * ext * tokens * dim * (heads + 2 * slots),
            bytes_accessed=14 * tokens * packed,
            transcendentals=ext * tokens * (heads + 2 * slots),
        ),
    )(reach, offs, q, k, v, g)


def on_device(mesh, query_tok, key_tok, value_tok, grad_out, head_reach, tile_offset):
    _, rows_dev, width, packed = query_tok.shape
    heads = head_reach.shape[0]
    group = 2 if heads % 2 == 0 else 1
    flat = [x.reshape(rows_dev * width, packed) for x in (query_tok, key_tok, value_tok, grad_out)]
    all_pairs = heads // group
    sizes = SIZES(all_pairs)
    branch = jnp.sum(head_reach) + (group - 1 - group * sizes[0])
    if group == 2:
        branch = lax.shift_right_arithmetic(branch, jnp.int32(1))
    run = [functools.partial(attention, mesh, size, group, width, heads) for size in sizes]
    if len(run) == 1:
        outs = run[0](head_reach, tile_offset.T, *flat)
    else:
        outs = lax.switch(branch, run, head_reach, tile_offset.T, *flat)
    return tuple(x.reshape(query_tok.shape) for x in in_head_order(head_reach, outs))


def SIZES(all_pairs):
    return list(range(max(all_pairs // 2 - 1, 0), all_pairs + 1))


def solution(mesh):
    tok = P("frame", "row", None, None)
    return jax.shard_map(
        functools.partial(on_device, mesh),
        mesh=mesh,
        in_specs=(tok, tok, tok, tok, P(), P(None, "row")),
        out_specs=(tok, tok, tok),
        check_vma=False,
    )
```
